32 devices in a mesh: seq: 4 (over y, x), tensor: 8 (over z, core).
Axes of the slice: x: 2, y: 2, z: 4, core: 2. Of those that a mesh axis runs over, the one named last changes fastest.
Arguments:
- queries: bfloat16 [4096, 4096], P(('seq', 'tensor')), may hold values from -6 to 6
- key_rows: bfloat16 [4096, 4096], P(('seq', 'tensor')), may hold values from -6 to 6
- values: bfloat16 [4096, 4096], P(('seq', 'tensor')), may hold values from -6 to 6
- input_gate: bfloat16 [4096, 4], P(('seq', 'tensor')), may hold values from -3 to 1
- forget_gate: bfloat16 [4096, 4], P(('seq', 'tensor')), may hold values from 0 to 16
- segment_ids: int32 [4096], P('seq'), may hold values from 0 to 3, never falling along the last dimension, each value on 1 to 2048 neighbouring positions
- output_gate: bfloat16 [4096, 4096], P(('seq', 'tensor')), may hold values from -6 to 6
- norm_gain: float32 [4096], replicated, may hold values from 0.5 to 1.5
Outputs:
- gated_out: bfloat16 [4096, 4096], P(('seq', 'tensor'))
The draws below stay inside these ranges and needn't reach their ends.
Inputs may be any that keep to these rules, and one draw needn't show every extreme that they name: `segment_ids`: non-decreasing along the tokens; each of the 4 prompts holds 1 to 2048 consecutive tokens, one exactly 2048.
All inputs are finite; a program needn't handle non-finite values.
Results may differ from the reference program's by a relative error of at most 0.005.
Values may be sent and summed in bfloat16 or wider, within the bound.
A program may use at most 64 MiB of HBM per device.

```python
import math
import jax
import jax.numpy as jnp
import numpy as np
from jax import lax

HEADS = 4
HEAD_DIM = 1024
INNER = 4096
TOK_DEV = 1024
BLOCK = 256
PROMPTS = 4
PACKED_TOKENS = 4096
MAX_LEN = 2048


def draw_forget_gate(key, part):
    key_order = jax.random.fold_in(key, 101)
    key_rough = jax.random.fold_in(key, 202)
    key_block = jax.random.fold_in(key, 303)
    key_spike = jax.random.fold_in(key, 404)
    order = jax.random.permutation(key_order, HEADS)
    slow_count = HEADS // 2
    sluggish_part = (order < slow_count).astype(jnp.float32)
    rough = jnp.exp(jax.random.uniform(key_rough, (PACKED_TOKENS, HEADS), jnp.float32, -0.7, 0.7))
    block_count = PACKED_TOKENS // TOK_DEV
    block_factor = jnp.exp(jax.random.uniform(key_block, (block_count, 1, HEADS), jnp.float32, -0.7, 0.7))
    block_factor = jnp.broadcast_to(block_factor, (block_count, TOK_DEV, HEADS)).reshape(PACKED_TOKENS, HEADS)
    base_rate = sluggish_part * (1.6 / PACKED_TOKENS) + (1.0 - sluggish_part) * (1.0 / 40.0)
    decay_rate = base_rate[None, :] * rough * block_factor
    token_positions = jax.random.randint(key_spike, (6,), 0, PACKED_TOKENS)
    spike_amount = jnp.any(jnp.arange(PACKED_TOKENS)[:, None] == token_positions[None, :], axis=1)
    decay_rate = jnp.where(spike_amount[:, None], sluggish_part[None, :] * 0.33 + (1.0 - sluggish_part[None, :]) * decay_rate, decay_rate)
    return jnp.log((1.0 - decay_rate) / decay_rate).astype(jnp.bfloat16)


def block_levels(rng, extent, pieces, low, high):
    factor_of = 1.0
    for dim, shards_of in pieces:
        heights = jax.random.uniform(jax.random.fold_in(jax.random.fold_in(rng, 6), dim), (shards_of,), jnp.float32, low / len(pieces), high / len(pieces))
        factor_of = factor_of * jnp.repeat(jnp.exp(heights), extent[dim] // shards_of).reshape((-1,) + (1,) * (len(extent) - 1 - dim))
    return factor_of


def split_up(amount, total, reach, skew):
    weights = [(1 << 20) // math.isqrt(standing ** skew) + 1 for standing in range(2, amount + 1)]
    surplus, given = total - reach - (amount - 1), [1] * (amount - 1)
    while surplus > 0:
        free = [i for i in range(amount - 1) if given[i] < reach]
        mass, remaining = sum([weights[i] for i in free]), surplus
        for i in free:
            more = min(reach - given[i], max(1, remaining * weights[i] // mass), surplus)
            given[i] = given[i] + more
            surplus = surplus - more
    return np.array([reach] + given)


def uneven_parts(stream_key, amount, total, limit, slope):
    if amount == 2:
        one = jax.random.randint(stream_key, (), max(1, total - limit), min(limit, total - 1) + 1)
        return jnp.stack([one, total - one])
    tallies = jnp.asarray(split_up(amount, total, limit, slope), jnp.int32)
    couples = (amount - 1) // 2
    giver, sink = tallies[1:1 + 2 * couples:2], tallies[2:2 + 2 * couples:2]
    room = jnp.minimum(giver - 1, limit - sink)
    shifted = jax.random.randint(jax.random.fold_in(stream_key, 1), (couples,), 0, 1 << 20) % (room + 1)
    tallies = tallies.at[1:1 + 2 * couples:2].set(giver - shifted).at[2:2 + 2 * couples:2].set(sink + shifted)
    return tallies[jax.random.permutation(jax.random.fold_in(stream_key, 2), amount)]


def normal_values(stream_key, shape, spread, bound, shards=(), kind=jnp.bfloat16):
    gain = block_levels(stream_key, shape, shards, -0.22, 0.18) if shards else 1.0
    drawn = jax.random.normal(stream_key, shape, jnp.float32) * spread * gain
    return jnp.minimum(jnp.maximum(drawn, -bound), bound).astype(kind)


def setup_inputs(seed: int = 0) -> dict:
    seeds = jax.random.split(jax.random.key(seed), 9)
    return {
        "queries": normal_values(seeds[0], (PACKED_TOKENS, INNER), 1.0, 6.0, ((0, 32),)),
        "key_rows": normal_values(seeds[1], (PACKED_TOKENS, INNER), 1.0, 6.0, ((0, 32),)),
        "values": normal_values(seeds[2], (PACKED_TOKENS, INNER), 1.0, 6.0, ((0, 32),)),
        "input_gate": jnp.clip(-3.0 + 4.0 * jax.random.uniform(seeds[3], (PACKED_TOKENS, HEADS), jnp.float32) ** block_levels(seeds[3], (PACKED_TOKENS, HEADS), ((0, 32),), -0.2, 0.2), -3.0, 1.0).astype(jnp.bfloat16),
        "forget_gate": draw_forget_gate(jax.random.fold_in(seeds[8], 71), 0),
        "segment_ids": jnp.searchsorted(jnp.cumsum(uneven_parts(seeds[5], PROMPTS, PACKED_TOKENS, MAX_LEN, 2)), jnp.arange(PACKED_TOKENS), side="right").astype(jnp.int32),
        "output_gate": normal_values(seeds[6], (PACKED_TOKENS, INNER), 1.0, 6.0, ((0, 32),)),
        "norm_gain": jnp.clip(1.0 + 0.1 * jax.random.normal(seeds[7], (INNER,), jnp.float32), 0.5, 1.5),
    }


precise = lax.Precision.HIGHEST

def reference(queries, key_rows, values, input_gate, forget_gate, segment_ids, output_gate, norm_gain):
    key_scale = 1.0 / math.sqrt(HEAD_DIM)
    blocks_all = PACKED_TOKENS // BLOCK
    query_float = queries.astype(jnp.float32).reshape(blocks_all, BLOCK, HEADS, HEAD_DIM)
    keys_f = key_rows.astype(jnp.float32).reshape(blocks_all, BLOCK, HEADS, HEAD_DIM) * key_scale
    values_f = values.astype(jnp.float32).reshape(blocks_all, BLOCK, HEADS, HEAD_DIM)
    gate_in = input_gate.astype(jnp.float32).reshape(blocks_all, BLOCK, HEADS)
    log_forget = jax.nn.log_sigmoid(forget_gate.astype(jnp.float32)).reshape(blocks_all, BLOCK, HEADS)
    segments = segment_ids.reshape(blocks_all, BLOCK)
    row_ids = jnp.arange(BLOCK, dtype=jnp.int32)
    causal = row_ids[:, None] >= row_ids[None, :]

    def span_step(carry, block_in):
        cell_state, norm_vec, prev_seg = carry
        query_b, key_b, value_b, gate_b, forget_b, seg_b = block_in
        cumulative = jnp.cumsum(forget_b, axis=0)
        allowed = (causal & (seg_b[:, None] == seg_b[None, :]))[None]
        cum_heads = cumulative.T
        exponent = cum_heads[:, :, None] - cum_heads[:, None, :] + gate_b.T[:, None, :]
        weights = jnp.where(allowed, jnp.exp(jnp.where(allowed, exponent, 0.0)), 0.0)
        scores = jnp.einsum('ihd,jhd->hij', query_b, key_b, precision=precise)
        weighted = weights * scores
        numerator = jnp.einsum('hij,jhd->ihd', weighted, value_b, precision=precise)
        q_norm = lax.optimization_barrier(jnp.sum(weighted, axis=2)).T
        carried = jnp.exp(cumulative) * (seg_b == prev_seg).astype(jnp.float32)[:, None]
        numerator = numerator + carried[:, :, None] * jnp.einsum('ihk,hkd->ihd', query_b, cell_state, precision=precise)
        q_norm = q_norm + carried * jnp.einsum('ihk,hk->ih', query_b, norm_vec, precision=precise)
        last_seg = seg_b[BLOCK - 1]
        tail_weight = jnp.exp(cumulative[BLOCK - 1][None, :] - cumulative + gate_b) * (seg_b == last_seg).astype(jnp.float32)[:, None]
        keep_factor = jnp.exp(cumulative[BLOCK - 1]) * (last_seg == prev_seg).astype(jnp.float32)
        scaled_keys = key_b * tail_weight[:, :, None]
        cell_state = keep_factor[:, None, None] * cell_state + jnp.einsum('jhk,jhd->hkd', scaled_keys, value_b, precision=precise)
        norm_vec = keep_factor[:, None] * norm_vec + lax.optimization_barrier(jnp.sum(scaled_keys, axis=0))
        hidden = (numerator / jnp.maximum(jnp.abs(q_norm), 1.0)[:, :, None]).astype(jnp.bfloat16)
        return ((cell_state, norm_vec, last_seg), hidden)
    initial = (jnp.zeros((HEADS, HEAD_DIM, HEAD_DIM), jnp.float32), jnp.zeros((HEADS, HEAD_DIM), jnp.float32), jnp.array(-1, jnp.int32))
    unused, hidden = lax.scan(span_step, initial, (query_float, keys_f, values_f, gate_in, log_forget, segments))
    hidden_f = hidden.astype(jnp.float32).reshape(PACKED_TOKENS, HEADS, HEAD_DIM)
    mean_val = lax.optimization_barrier(jnp.mean(hidden_f, axis=2, keepdims=True))
    centered = hidden_f - mean_val
    variance = lax.optimization_barrier(jnp.mean(centered * centered, axis=2, keepdims=True))
    normed = (centered * lax.rsqrt(variance + 1e-05)).reshape(PACKED_TOKENS, INNER)
    return (normed * norm_gain * jax.nn.silu(output_gate.astype(jnp.float32))).astype(jnp.bfloat16)
```

```python
import functools
import math

import jax
import jax.numpy as jnp
from jax import lax
from jax.experimental import pallas as pl
from jax.experimental.pallas import tpu as pltpu
from jax.sharding import PartitionSpec as P

MESH = pl.DeviceIdType.MESH
F32 = jnp.float32
BF16 = jnp.bfloat16
EPS = 1e-05
TILE = 256
NONE = -1e30


def send(src, dst, send_sem, recv_sem, axis, index):
    return pltpu.make_async_remote_copy(
        src_ref=src,
        dst_ref=dst,
        send_sem=send_sem,
        recv_sem=recv_sem,
        device_id={axis: index},
        device_id_type=MESH,
    )


def kernel(
    dims,
    gates_ref,
    seg_ref,
    gain_ref,
    q_ref,
    k_ref,
    v_ref,
    og_ref,
    out_ref,
    gates_all,
    k_all,
    v_all,
    q_all,
    vt,
    lf_col,
    gate_col,
    cum_col,
    seg_col,
    tail_col,
    rows,
    meta,
    meta_all,
    tot,
    pre,
    pre_bf,
    stage,
    relay,
    tot_n,
    pre_n,
    stage_n,
    relay_n,
    num,
    qn,
    hid,
    out_rx,
    og_v,
    g_send,
    g_recv,
    k_send,
    k_fwd,
    k_recv,
    v_send,
    v_recv,
    q_send,
    q_fwd,
    q_recv,
    m_send,
    m_recv,
    r_send,
    r_recv,
    n_send,
    n_recv,
    o_send,
    o_recv,
    og_sem,
):
    seq_n, ten_n, heads, R, D = dims
    group = ten_n // heads
    C = D // group
    N = ten_n * R
    B = min(TILE, N)
    nb = N // B
    per = B // R
    chunk = min(256, D)
    nc = D // chunk
    levels = seq_n.bit_length() - 1
    scale = 1.0 / math.sqrt(D)
    t = lax.axis_index("tensor")
    s = lax.axis_index("seq")
    h = lax.div(t, group)
    m = lax.rem(t, group)

    def block(index):
        return pl.ds(pl.multiple_of(index * R, R), R)

    def tile(index):
        return pl.ds(pl.multiple_of(index * B, B), B)

    def head_cols(index):
        return pl.ds(pl.multiple_of(index * D, 128), D)

    def val_cols(index):
        return pl.ds(pl.multiple_of(index * C, 128), C)

    barrier = pltpu.get_barrier_semaphore()
    for d in range(1, ten_n):
        pl.semaphore_signal(
            barrier, inc=1, device_id={"tensor": lax.rem(t + d, ten_n)}, device_id_type=MESH
        )
    for d in range(1, seq_n):
        pl.semaphore_signal(
            barrier, inc=1, device_id={"seq": lax.rem(s + d, seq_n)}, device_id_type=MESH
        )
    pl.semaphore_wait(barrier, ten_n + seq_n - 2)

    def gate_copy(d):
        return send(
            gates_ref, gates_all.at[t], g_send.at[d - 1], g_recv.at[t], "tensor", lax.rem(t + d, ten_n)
        )

    def head_copy(src, dst, sem, rsem, d):
        hh = lax.rem(h + d, heads)
        return send(
            src.at[:, head_cols(hh)], dst.at[block(t)], sem.at[d - 1], rsem.at[t], "tensor", hh * group + m
        )

    def own_copy(src, dst, rsem):
        return pltpu.make_async_copy(src.at[:, head_cols(h)], dst.at[block(t)], rsem.at[t])

    def own_forward(src, dst, sem, rsem, g):
        return send(
            src.at[:, head_cols(h)],
            dst.at[block(t)],
            sem.at[g - 1],
            rsem.at[t],
            "tensor",
            h * group + lax.rem(m + g, group),
        )

    def source_block(d):
        return lax.rem(h + heads - d, heads) * group + m

    def forward(dst, sem, rsem, d, g):
        b = source_block(d)
        return send(
            dst.at[block(b)],
            dst.at[block(b)],
            sem.at[d * (group - 1) + g - 1],
            rsem.at[b],
            "tensor",
            h * group + lax.rem(m + g, group),
        )

    def arrive(dst, rsem, sem, b):
        send(dst.at[block(b)], dst.at[block(b)], sem.at[0], rsem.at[b], "tensor", lax.rem(t + 1, ten_n)).wait_recv()

    def val_copy(d):
        tt = lax.rem(t + d, ten_n)
        return send(
            v_ref.at[:, val_cols(tt)], v_all.at[block(t)], v_send.at[d - 1], v_recv.at[t], "tensor", tt
        )

    for d in range(1, ten_n):
        gate_copy(d).start()
    gates_all[t] = gates_ref[...]
    for d in range(1, heads):
        head_copy(k_ref, k_all, k_send, k_recv, d).start()
    own_copy(k_ref, k_all, k_recv).start()
    for g in range(1, group):
        own_forward(k_ref, k_all, k_fwd, k_recv, g).start()
    for d in range(1, ten_n):
        val_copy(d).start()
    own_val = pltpu.make_async_copy(v_ref.at[:, val_cols(t)], v_all.at[block(t)], v_recv.at[t])
    own_val.start()
    for d in range(1, heads):
        head_copy(q_ref, q_all, q_send, q_recv, d).start()
    own_copy(q_ref, q_all, q_recv).start()
    for g in range(1, group):
        own_forward(q_ref, q_all, q_fwd, q_recv, g).start()
    og_copy = pltpu.make_async_copy(og_ref, og_v, og_sem)
    og_copy.start()

    for d in range(1, ten_n):
        b = lax.rem(t + ten_n - d, ten_n)
        send(
            gates_ref, gates_all.at[b], g_send.at[0], g_recv.at[b], "tensor", lax.rem(t + 1, ten_n)
        ).wait_recv()
    eye_r = lax.broadcasted_iota(jnp.int32, (R, R), 0) == lax.broadcasted_iota(jnp.int32, (R, R), 1)

    def spread_gates(b, carry):
        both = gates_all[b]
        line = lax.broadcasted_iota(jnp.int32, both.shape, 0)
        gate_in = jnp.sum(jnp.where(line == h, both, 0.0), axis=0, keepdims=True)[:, :R]
        pre_f = jnp.sum(jnp.where(line == h + heads, both, 0.0), axis=0, keepdims=True)[:, :R]
        log_f = jnp.minimum(pre_f, 0.0) - jnp.log1p(jnp.exp(-jnp.abs(pre_f)))
        to_col = lambda row: jnp.broadcast_to(
            jnp.sum(jnp.where(eye_r, jnp.broadcast_to(row, (R, R)), 0.0), axis=1, keepdims=True), (R, 128)
        )
        lf_col[block(b)] = to_col(log_f)
        gate_col[block(b)] = to_col(gate_in)
        return carry

    lax.fori_loop(0, ten_n, spread_gates, 0)
    row_i = lax.broadcasted_iota(jnp.int32, (B, B), 0)
    col_i = lax.broadcasted_iota(jnp.int32, (B, B), 1)
    eye = row_i == col_i

    def as_row(mask, col):
        return jnp.sum(jnp.where(mask, jnp.broadcast_to(col, (B, B)), 0.0), axis=0, keepdims=True)

    def as_col(row):
        return jnp.broadcast_to(
            jnp.sum(jnp.where(eye, jnp.broadcast_to(row, (B, B)), 0.0), axis=1, keepdims=True), (B, 128)
        )

    total = jnp.zeros((1, 1), F32)
    for b in range(nb):
        here = pl.ds(b * B, B)
        cum = as_row(row_i <= col_i, lf_col[here, 0:1]) + total
        total = cum[:, B - 1 : B]
        rows[b, 0:1, :] = cum
        rows[b, 1:2, :] = as_row(eye, gate_col[here, 0:1]) - cum
        rows[b, 2:3, :] = seg_ref[b : b + 1, :]
        cum_col[here] = as_col(cum)
        seg_col[here] = as_col(seg_ref[b : b + 1, :])
    first_seg = seg_ref[0:1, 0:1]
    last_seg = seg_ref[nb - 1 : nb, B - 1 : B]
    for b in range(nb):
        here = pl.ds(b * B, B)
        kept = rows[b, 2:3, :] == last_seg
        tail = jnp.where(kept, jnp.exp(total + rows[b, 1:2, :]) * scale, 0.0)
        rows[b, 3:4, :] = tail
        tail_col[here] = as_col(tail)
    meta[0:1, :] = jnp.broadcast_to(total, (1, 128))
    meta[1:2, :] = jnp.broadcast_to(first_seg, (1, 128))
    meta[2:8, :] = jnp.broadcast_to(last_seg, (6, 128))

    def meta_copy(d):
        return send(
            meta, meta_all.at[s], m_send.at[d - 1], m_recv.at[s], "seq", lax.rem(s + d, seq_n)
        )

    for d in range(1, seq_n):
        meta_copy(d).start()
    meta_all[s] = meta[...]

    for d in range(1, heads):
        arrive(k_all, k_recv, k_send, source_block(d))
        for g in range(1, group):
            forward(k_all, k_fwd, k_recv, d, g).start()
    for d in range(1, ten_n):
        arrive(v_all, v_recv, v_send, lax.rem(t + ten_n - d, ten_n))
    own_val.wait()

    def scale_values(b, carry):
        vt[tile(b)] = (v_all[tile(b)].astype(F32) * tail_col[tile(b), 0:1]).astype(BF16)
        return carry

    lax.fori_loop(0, nb, scale_values, 0)
    own_copy(k_ref, k_all, k_recv).wait()
    for g in range(1, group):
        for hh in range(heads):
            arrive(k_all, k_recv, k_send, hh * group + lax.rem(m + g, group))

    def chunk_rows(c):
        return pl.ds(pl.multiple_of(c * chunk, chunk), chunk)

    def relay_copy(level, c):
        return send(
            stage.at[level, chunk_rows(c)],
            relay.at[level, chunk_rows(c)],
            r_send.at[level, c],
            r_recv.at[level, c],
            "seq",
            s + (1 - 2 * lax.rem(lax.div(s, 1 << level), 2)) * (1 << level),
        )

    def norm_copy(level):
        return send(
            stage_n.at[level],
            relay_n.at[level],
            n_send.at[level],
            n_recv.at[level],
            "seq",
            s + (1 - 2 * lax.rem(lax.div(s, 1 << level), 2)) * (1 << level),
        )

    def make_state(c, carry):
        part = lax.dot_general(
            k_all[:, pl.ds(pl.multiple_of(c * chunk, 128), chunk)],
            vt[...],
            (((0,), (0,)), ((), ())),
            preferred_element_type=F32,
        )
        tot[chunk_rows(c)] = part
        stage[0, chunk_rows(c)] = part.astype(BF16)
        relay_copy(0, c).start()
        return carry

    lax.fori_loop(0, nc, make_state, 0)
    tot_n[...] = jnp.zeros_like(tot_n)

    def add_norm(b, carry):
        tail = jnp.broadcast_to(rows[b][3:4, :], (16, B))
        line = lax.broadcasted_iota(jnp.int32, (16, B), 0)
        high = tail.astype(BF16).astype(F32)
        two = jnp.where(line == 0, high, jnp.where(line == 1, tail - high, 0.0)).astype(BF16)
        part = jnp.dot(two, k_all[tile(b)], preferred_element_type=F32)
        tot_n[...] += jnp.broadcast_to(part[0:1] + part[1:2], tot_n.shape)
        return carry

    lax.fori_loop(0, nb, add_norm, 0)
    stage_n[0] = tot_n[...]
    norm_copy(0).start()

    for d in range(1, seq_n):
        b = lax.rem(s + seq_n - d, seq_n)
        send(
            meta, meta_all.at[b], m_send.at[0], m_recv.at[b], "seq", lax.rem(s + 1, seq_n)
        ).wait_recv()

    def factors(level):
        width = 1 << level
        upper = lax.rem(lax.div(s, width), 2)
        base = lax.div(s, 2 * width) * (2 * width)
        low_end = base + width - 1
        high_end = base + 2 * width - 1
        to_here = jnp.zeros((1, 128), F32)
        to_end = jnp.zeros((1, 128), F32)
        for u in range(seq_n):
            log_u = meta_all[u][0:1, :]
            to_here = to_here + jnp.where((u > low_end) & (u < s), log_u, 0.0)
            to_end = to_end + jnp.where((u > low_end) & (u <= high_end), log_u, 0.0)
        low_last = meta_all[low_end][2:3, :]
        here = jnp.where(low_last == first_seg, jnp.exp(to_here), 0.0)
        end = jnp.where(low_last == meta_all[high_end][2:3, :], jnp.exp(to_end), 0.0)
        here = jnp.where(upper == 1, here, 0.0)[:, 0:1]
        own = jnp.where(upper == 1, 1.0, end)[:, 0:1]
        other = jnp.where(upper == 1, end, 1.0)[:, 0:1]
        return here, own, other

    def relay_level(level, between):
        here, own, other = factors(level)

        def join(c):
            relay_copy(level, c).wait_recv()
            got = relay[level, chunk_rows(c)].astype(F32)
            if level == 0:
                fresh = here * got
            else:
                fresh = pre[chunk_rows(c)] + here * got
            if level < levels - 1:
                pre[chunk_rows(c)] = fresh
                joined = own * tot[chunk_rows(c)] + other * got
                tot[chunk_rows(c)] = joined
                stage[level + 1, chunk_rows(c)] = joined.astype(BF16)
                relay_copy(level + 1, c).start()
            else:
                pre_bf[chunk_rows(c)] = fresh.astype(BF16)

        for c in range(nc):
            between(c)
            join(c)
        norm_copy(level).wait_recv()
        got = relay_n[level]
        if level == 0:
            pre_n[...] = here * got
        else:
            pre_n[...] = pre_n[...] + here * got
        if level < levels - 1:
            joined = own * tot_n[...] + other * got
            tot_n[...] = joined
            stage_n[level + 1] = joined
            norm_copy(level + 1).start()

    def take_query(d):
        if 1 <= d < heads:
            arrive(q_all, q_recv, q_send, source_block(d))
            for g in range(1, group):
                forward(q_all, q_fwd, q_recv, d, g).start()

    relay_level(0, lambda c: take_query(c))
    for d in range(nc, heads):
        take_query(d)
    own_copy(q_ref, q_all, q_recv).wait()
    for g in range(1, group):
        for hh in range(heads):
            arrive(q_all, q_recv, q_send, hh * group + lax.rem(m + g, group))

    def query_tile(i, carry):
        num[tile(i)] = jnp.zeros((B, C), F32)
        qn[tile(i)] = jnp.zeros((B, 128), F32)

        def key_tile(j, inner):
            scores = lax.dot_general(
                q_all[tile(i)], k_all[tile(j)], (((1,), (1,)), ((), ())), preferred_element_type=F32
            )
            row = rows[j]
            allowed = (i * B + row_i >= j * B + col_i) & (seg_col[tile(i), 0:1] == row[2:3, :])
            exponent = jnp.where(allowed, cum_col[tile(i), 0:1] + row[1:2, :], NONE)
            weighted = jnp.exp(exponent) * (scores * scale)
            qn[tile(i)] += jnp.broadcast_to(jnp.sum(weighted, axis=1, keepdims=True), (B, 128))
            num[tile(i)] += jnp.dot(weighted.astype(BF16), v_all[tile(j)], preferred_element_type=F32)
            return inner

        return lax.fori_loop(0, i + 1, key_tile, carry)

    lax.fori_loop(0, nb, query_tile, 0)
    for level in range(1, levels):
        relay_level(level, lambda c: None)

    line = lax.broadcasted_iota(jnp.int32, (16, D), 0)
    norm_row = jnp.broadcast_to(pre_n[0:1, :], (16, D))
    norm_high = norm_row.astype(BF16).astype(F32)
    norm_two = jnp.where(
        line == 0, norm_high, jnp.where(line == 1, norm_row - norm_high, 0.0)
    ).astype(BF16)
    pre_two = norm_two
    my_tile = lax.div(t, per)

    def out_copy(b):
        return send(hid.at[block(b)], out_rx.at[t], o_send.at[b], o_recv.at[t], "tensor", b)

    def own_out():
        return pltpu.make_async_copy(hid.at[block(t)], out_rx.at[t], o_recv.at[t])

    def finish_tile(step, carry):
        i = lax.rem(my_tile + 1 + step, nb)
        query = q_all[tile(i)]
        entry = jnp.where(
            seg_col[tile(i), 0:1] == first_seg, jnp.exp(cum_col[tile(i), 0:1]), 0.0
        )
        carried = jnp.dot(query, pre_bf[...], preferred_element_type=F32)
        carried_n = jnp.sum(
            lax.dot_general(query, pre_two, (((1,), (1,)), ((), ())), preferred_element_type=F32),
            axis=1,
            keepdims=True,
        )
        bottom = qn[tile(i), 0:1] + entry * carried_n
        top = num[tile(i)] + entry * carried
        hid[tile(i)] = (top / jnp.maximum(jnp.abs(bottom), 1.0)).astype(BF16)
        for p in range(per):
            b = i * per + p

            @pl.when(b != t)
            def _():
                out_copy(b).start()

            @pl.when(b == t)
            def _():
                own_out().start()

        return carry

    lax.fori_loop(0, nb, finish_tile, 0)

    og_copy.wait()
    own_out().wait()

    def finish_head(step, carry):
        hh = lax.rem(h + step, heads)
        parts = []
        for g in range(group):
            b = hh * group + g

            @pl.when(b != t)
            def _():
                send(
                    hid.at[block(b)], out_rx.at[b], o_send.at[b], o_recv.at[b], "tensor", lax.rem(t + 1, ten_n)
                ).wait_recv()

            parts.append(out_rx[b].astype(F32))
        mean = sum(jnp.sum(x, axis=1, keepdims=True) for x in parts) * (1.0 / D)
        parts = [x - mean for x in parts]
        var = sum(jnp.sum(x * x, axis=1, keepdims=True) for x in parts) * (1.0 / D)
        inv = lax.rsqrt(var + EPS)
        for g in range(group):
            cols = val_cols(hh * group + g)
            gate = og_v[:, cols].astype(F32)
            silu = gate / (1.0 + jnp.exp(-gate))
            out_ref[:, cols] = (parts[g] * inv * gain_ref[:, cols] * silu).astype(BF16)
        return carry

    lax.fori_loop(0, heads, finish_head, 0)

    for d in range(1, ten_n):
        gate_copy(d).wait_send()
        val_copy(d).wait_send()
        out_copy(lax.rem(t + d, ten_n)).wait_send()
    for d in range(1, heads):
        head_copy(k_ref, k_all, k_send, k_recv, d).wait_send()
        head_copy(q_ref, q_all, q_send, q_recv, d).wait_send()
    for g in range(1, group):
        own_forward(k_ref, k_all, k_fwd, k_recv, g).wait_send()
        own_forward(q_ref, q_all, q_fwd, q_recv, g).wait_send()
        for d in range(1, heads):
            forward(k_all, k_fwd, k_recv, d, g).wait_send()
            forward(q_all, q_fwd, q_recv, d, g).wait_send()
    for d in range(1, seq_n):
        meta_copy(d).wait_send()
    for level in range(levels):
        norm_copy(level).wait_send()
        for c in range(nc):
            relay_copy(level, c).wait_send()


def on_device(
    seq_n, ten_n, queries, key_rows, values, input_gate, forget_gate, segment_ids, output_gate, norm_gain
):
    R, inner = queries.shape
    heads = input_gate.shape[1]
    D = inner // heads
    group = ten_n // heads
    C = D // group
    N = ten_n * R
    B = min(TILE, N)
    nb = N // B
    nc = D // min(256, D)
    levels = seq_n.bit_length() - 1
    gates = jnp.concatenate([input_gate, forget_gate], axis=1).astype(F32).T
    lanes = max(R, 128)
    gates = jnp.pad(gates, ((0, -(2 * heads) % 8), (0, lanes - R)))
    lines = gates.shape[0]
    segs = segment_ids.astype(F32).reshape(nb, B)
    dma = pltpu.SemaphoreType.DMA
    vmem = pltpu.VMEM
    whole = pl.BlockSpec(memory_space=pltpu.VMEM)
    far = pl.BlockSpec(memory_space=pl.ANY)
    forwards = max(1, heads * (group - 1))
    return pl.pallas_call(
        functools.partial(kernel, (seq_n, ten_n, heads, R, D)),
        out_shape=jax.ShapeDtypeStruct((R, inner), BF16),
        in_specs=[whole, whole, whole, far, far, far, far],
        out_specs=whole,
        scratch_shapes=[
            vmem((ten_n, lines, lanes), F32),
            vmem((N, D), BF16),
            vmem((N, C), BF16),
            vmem((N, D), BF16),
            vmem((N, C), BF16),
            vmem((N, 128), F32),
            vmem((N, 128), F32),
            vmem((N, 128), F32),
            vmem((N, 128), F32),
            vmem((N, 128), F32),
            vmem((nb, 8, B), F32),
            vmem((8, 128), F32),
            vmem((seq_n, 8, 128), F32),
            vmem((D, C), F32),
            vmem((D, C), F32),
            vmem((D, C), BF16),
            vmem((levels, D, C), BF16),
            vmem((levels, D, C), BF16),
            vmem((8, D), F32),
            vmem((8, D), F32),
            vmem((levels, 8, D), F32),
            vmem((levels, 8, D), F32),
            vmem((N, C), F32),
            vmem((N, 128), F32),
            vmem((N, C), BF16),
            vmem((ten_n, R, C), BF16),
            vmem((R, inner), BF16),
            dma((ten_n,)),
            dma((ten_n,)),
            dma((heads,)),
            dma((forwards,)),
            dma((ten_n,)),
            dma((ten_n,)),
            dma((ten_n,)),
            dma((heads,)),
            dma((forwards,)),
            dma((ten_n,)),
            dma((seq_n,)),
            dma((seq_n,)),
            dma((levels, nc)),
            dma((levels, nc)),
            dma((levels,)),
            dma((levels,)),
            dma((ten_n,)),
            dma((ten_n,)),
            dma,
        ],
        compiler_params=pltpu.CompilerParams(
            collective_id=0, has_side_effects=True, vmem_limit_bytes=48 * 1024 * 1024
        ),
        cost_estimate=pl.CostEstimate(
            flops=2 * N * (N * D + N * C + 2 * D * C), bytes_accessed=10 * R * inner, transcendentals=N * N
        ),
    )(gates, segs, norm_gain.reshape(1, inner), queries, key_rows, values, output_gate)


def solution(mesh):
    rows = P(("seq", "tensor"), None)
    return jax.shard_map(
        functools.partial(on_device, mesh.shape["seq"], mesh.shape["tensor"]),
        mesh=mesh,
        in_specs=(rows, rows, rows, rows, rows, P("seq"), rows, P()),
        out_specs=rows,
        check_vma=False,
    )
```

```python
import functools
import math

import jax
import jax.numpy as jnp
from jax import lax
from jax.experimental import pallas as pl
from jax.experimental.pallas import tpu as pltpu
from jax.sharding import PartitionSpec as P

MESH = pl.DeviceIdType.MESH
F32 = jnp.float32
BF16 = jnp.bfloat16
EPS = 1e-05
NONE = -1e30


def send(src, dst, send_sem, recv_sem, axis, index):
    return pltpu.make_async_remote_copy(
        src_ref=src,
        dst_ref=dst,
        send_sem=send_sem,
        recv_sem=recv_sem,
        device_id={axis: index},
        device_id_type=MESH,
    )


def kernel(
    dims,
    gates_ref,
    seg_ref,
    gain_ref,
    q_ref,
    k_ref,
    v_ref,
    og_ref,
    out_ref,
    gates_all,
    k_all,
    v_all,
    q_all,
    vt,
    lf_col,
    gate_col,
    cum_col,
    seg_col,
    tail_col,
    rows,
    meta,
    meta_all,
    tot,
    pre,
    pre_bf,
    stage,
    relay,
    tot_n,
    pre_n,
    stage_n,
    relay_n,
    num,
    qn,
    hid,
    out_rx,
    og_v,
    g_send,
    g_recv,
    k_send,
    k_fwd,
    k_recv,
    v_send,
    v_recv,
    q_send,
    q_fwd,
    q_recv,
    m_send,
    m_recv,
    r_send,
    r_recv,
    n_send,
    n_recv,
    o_send,
    o_recv,
    og_sem,
    k_own,
):
    seq_n, ten_n, heads, R, D = dims
    group = ten_n // heads
    C = D // group
    N = ten_n * R
    B = group * R
    nb = heads
    chunk = min(256, D)
    nc = D // chunk
    levels = seq_n.bit_length() - 1
    scale = 1.0 / math.sqrt(D)
    t = lax.axis_index("tensor")
    s = lax.axis_index("seq")
    h = lax.div(t, group)
    m = lax.rem(t, group)

    def block(index):
        return pl.ds(pl.multiple_of(index * R, R), R)

    def tile(index):
        return pl.ds(pl.multiple_of(index * B, B), B)

    def head_cols(index):
        return pl.ds(pl.multiple_of(index * D, 128), D)

    def val_cols(index):
        return pl.ds(pl.multiple_of(index * C, 128), C)

    barrier = pltpu.get_barrier_semaphore()
    for d in range(1, ten_n):
        pl.semaphore_signal(
            barrier, inc=1, device_id={"tensor": lax.rem(t + d, ten_n)}, device_id_type=MESH
        )
    for d in range(1, seq_n):
        pl.semaphore_signal(
            barrier, inc=1, device_id={"seq": lax.rem(s + d, seq_n)}, device_id_type=MESH
        )
    pl.semaphore_wait(barrier, ten_n + seq_n - 2)

    def gate_copy(d):
        return send(
            gates_ref, gates_all.at[t], g_send.at[d - 1], g_recv.at[t], "tensor", lax.rem(t + d, ten_n)
        )

    def head_copy(src, dst, sem, rsem, d):
        hh = lax.rem(h + d, heads)
        return send(
            src.at[:, head_cols(hh)], dst.at[block(t)], sem.at[d - 1], rsem.at[t], "tensor", hh * group + m
        )

    def own_copy(src, dst, rsem):
        return pltpu.make_async_copy(src.at[:, head_cols(h)], dst.at[block(t)], rsem.at[t])

    def own_forward(src, dst, sem, rsem, g):
        return send(
            src.at[:, head_cols(h)],
            dst.at[block(t)],
            sem.at[g - 1],
            rsem.at[t],
            "tensor",
            h * group + lax.rem(m + g, group),
        )

    def source_block(d):
        return lax.rem(h + heads - d, heads) * group + m

    def forward(dst, sem, rsem, d, g):
        b = source_block(d)
        return send(
            dst.at[block(b)],
            dst.at[block(b)],
            sem.at[d * (group - 1) + g - 1],
            rsem.at[b],
            "tensor",
            h * group + lax.rem(m + g, group),
        )

    def arrive(dst, rsem, sem, b):
        send(dst.at[block(b)], dst.at[block(b)], sem.at[0], rsem.at[b], "tensor", lax.rem(t + 1, ten_n)).wait_recv()

    def key_copy(d, c):
        hh = lax.rem(h + d, heads)
        return send(
            k_ref.at[:, pl.ds(pl.multiple_of(hh * D + c * chunk, 128), chunk)],
            k_all.at[block(t), pl.ds(c * chunk, chunk)],
            k_send.at[d - 1, c],
            k_recv.at[t, c],
            "tensor",
            hh * group + m,
        )

    def key_forward(d, g, c):
        b = source_block(d)
        here = k_all.at[block(b), pl.ds(c * chunk, chunk)]
        source = k_ref.at[:, pl.ds(pl.multiple_of(h * D + c * chunk, 128), chunk)] if d == 0 else here
        return send(
            source,
            here,
            k_fwd.at[d * (group - 1) + g - 1, c],
            k_recv.at[b, c],
            "tensor",
            h * group + lax.rem(m + g, group),
        )

    def key_arrive(b, c):
        here = k_all.at[block(b), pl.ds(c * chunk, chunk)]
        send(here, here, k_send.at[0, c], k_recv.at[b, c], "tensor", lax.rem(t + 1, ten_n)).wait_recv()

    def send_keys(c):
        for d in range(1, heads):
            key_copy(d, c).start()

    def send_queries(d):
        head_copy(q_ref, q_all, q_send, q_recv, d).start()

    def val_copy(d):
        tt = lax.rem(t + d, ten_n)
        return send(
            v_ref.at[:, val_cols(tt)], v_all.at[block(t)], v_send.at[d - 1], v_recv.at[t], "tensor", tt
        )

    for d in range(1, ten_n):
        gate_copy(d).start()
    gates_all[t] = gates_ref[...]
    for d in range(1, ten_n):
        val_copy(d).start()
    own_val = pltpu.make_async_copy(v_ref.at[:, val_cols(t)], v_all.at[block(t)], v_recv.at[t])
    own_val.start()
    own_key = pltpu.make_async_copy(k_ref.at[:, head_cols(h)], k_all.at[block(t)], k_own)
    own_key.start()
    own_copy(q_ref, q_all, q_recv).start()
    for g in range(1, group):
        for c in range(nc):
            key_forward(0, g, c).start()
        own_forward(q_ref, q_all, q_fwd, q_recv, g).start()
    queue = [functools.partial(send_keys, c) for c in range(nc)]
    queue += [functools.partial(send_queries, d) for d in range(1, heads)]

    def next_piece():
        if queue:
            queue.pop(0)()

    next_piece()
    next_piece()
    og_copy = pltpu.make_async_copy(og_ref, og_v, og_sem)
    og_copy.start()

    for d in range(1, ten_n):
        b = lax.rem(t + ten_n - d, ten_n)
        send(
            gates_ref, gates_all.at[b], g_send.at[0], g_recv.at[b], "tensor", lax.rem(t + 1, ten_n)
        ).wait_recv()
    eye_r = lax.broadcasted_iota(jnp.int32, (R, R), 0) == lax.broadcasted_iota(jnp.int32, (R, R), 1)

    def spread_gates(b, carry):
        both = gates_all[b]
        line = lax.broadcasted_iota(jnp.int32, both.shape, 0)
        gate_in = jnp.sum(jnp.where(line == h, both, 0.0), axis=0, keepdims=True)[:, :R]
        pre_f = jnp.sum(jnp.where(line == h + heads, both, 0.0), axis=0, keepdims=True)[:, :R]
        log_f = jnp.minimum(pre_f, 0.0) - jnp.log1p(jnp.exp(-jnp.abs(pre_f)))
        to_col = lambda row: jnp.broadcast_to(
            jnp.sum(jnp.where(eye_r, jnp.broadcast_to(row, (R, R)), 0.0), axis=1, keepdims=True), (R, 128)
        )
        lf_col[block(b)] = to_col(log_f)
        gate_col[block(b)] = to_col(gate_in)
        return carry

    lax.fori_loop(0, ten_n, spread_gates, 0)
    row_i = lax.broadcasted_iota(jnp.int32, (B, B), 0)
    col_i = lax.broadcasted_iota(jnp.int32, (B, B), 1)
    eye = row_i == col_i

    def as_row(mask, col):
        return jnp.sum(jnp.where(mask, jnp.broadcast_to(col, (B, B)), 0.0), axis=0, keepdims=True)

    def as_col(row):
        return jnp.broadcast_to(
            jnp.sum(jnp.where(eye, jnp.broadcast_to(row, (B, B)), 0.0), axis=1, keepdims=True), (B, 128)
        )

    def segs(b):
        return seg_ref[0:1, b * B : (b + 1) * B].astype(F32)

    total = jnp.zeros((1, 1), F32)
    for b in range(nb):
        here = pl.ds(b * B, B)
        cum = as_row(row_i <= col_i, lf_col[here, 0:1]) + total
        total = cum[:, B - 1 : B]
        rows[b, 0:1, :] = cum
        rows[b, 1:2, :] = as_row(eye, gate_col[here, 0:1]) - cum
        rows[b, 2:3, :] = segs(b)
        cum_col[here] = as_col(cum)
        seg_col[here] = as_col(segs(b))
    first_seg = segs(0)[:, 0:1]
    last_seg = segs(nb - 1)[:, B - 1 : B]
    for b in range(nb):
        here = pl.ds(b * B, B)
        kept = rows[b, 2:3, :] == last_seg
        tail = jnp.where(kept, jnp.exp(total + rows[b, 1:2, :]) * scale, 0.0)
        rows[b, 3:4, :] = tail
        tail_col[here] = as_col(tail)
    meta[0:1, :] = jnp.broadcast_to(total, (1, 128))
    meta[1:2, :] = jnp.broadcast_to(first_seg, (1, 128))
    meta[2:8, :] = jnp.broadcast_to(last_seg, (6, 128))

    def meta_copy(d):
        return send(
            meta, meta_all.at[s], m_send.at[d - 1], m_recv.at[s], "seq", lax.rem(s + d, seq_n)
        )

    for d in range(1, seq_n):
        meta_copy(d).start()
    meta_all[s] = meta[...]

    for d in range(1, ten_n):
        arrive(v_all, v_recv, v_send, lax.rem(t + ten_n - d, ten_n))
    own_val.wait()
    next_piece()

    def scale_values(b, carry):
        vt[tile(b)] = (v_all[tile(b)].astype(F32) * tail_col[tile(b), 0:1]).astype(BF16)
        return carry

    lax.fori_loop(0, nb, scale_values, 0)
    def chunk_rows(c):
        return pl.ds(pl.multiple_of(c * chunk, chunk), chunk)

    def relay_copy(level, c):
        return send(
            stage.at[level, chunk_rows(c)],
            relay.at[level, chunk_rows(c)],
            r_send.at[level, c],
            r_recv.at[level, c],
            "seq",
            s + (1 - 2 * lax.rem(lax.div(s, 1 << level), 2)) * (1 << level),
        )

    def norm_copy(level):
        return send(
            stage_n.at[level],
            relay_n.at[level],
            n_send.at[level],
            n_recv.at[level],
            "seq",
            s + (1 - 2 * lax.rem(lax.div(s, 1 << level), 2)) * (1 << level),
        )

    def make_state(c):
        part = lax.dot_general(
            k_all[:, pl.ds(c * chunk, chunk)], vt[...], (((0,), (0,)), ((), ())), preferred_element_type=F32
        )
        tot[chunk_rows(c)] = part
        stage[0, chunk_rows(c)] = part.astype(BF16)
        relay_copy(0, c).start()

    for d in range(1, seq_n):
        b = lax.rem(s + seq_n - d, seq_n)
        send(
            meta, meta_all.at[b], m_send.at[0], m_recv.at[b], "seq", lax.rem(s + 1, seq_n)
        ).wait_recv()

    def factors(level):
        width = 1 << level
        upper = lax.rem(lax.div(s, width), 2)
        base = lax.div(s, 2 * width) * (2 * width)
        low_end = base + width - 1
        high_end = base + 2 * width - 1
        to_here = jnp.zeros((1, 128), F32)
        to_end = jnp.zeros((1, 128), F32)
        for u in range(seq_n):
            log_u = meta_all[u][0:1, :]
            to_here = to_here + jnp.where((u > low_end) & (u < s), log_u, 0.0)
            to_end = to_end + jnp.where((u > low_end) & (u <= high_end), log_u, 0.0)
        low_last = meta_all[low_end][2:3, :]
        here = jnp.where(low_last == first_seg, jnp.exp(to_here), 0.0)
        end = jnp.where(low_last == meta_all[high_end][2:3, :], jnp.exp(to_end), 0.0)
        here = jnp.where(upper == 1, here, 0.0)[:, 0:1]
        own = jnp.where(upper == 1, 1.0, end)[:, 0:1]
        other = jnp.where(upper == 1, end, 1.0)[:, 0:1]
        return here, own, other

    links = [factors(level) for level in range(levels)]

    def join(level, c):
        here, own, other = links[level]
        relay_copy(level, c).wait_recv()
        got = relay[level, chunk_rows(c)].astype(F32)
        fresh = here * got
        if level > 0:
            fresh = pre[chunk_rows(c)] + fresh
        if level < levels - 1:
            pre[chunk_rows(c)] = fresh
            joined = own * tot[chunk_rows(c)] + other * got
            tot[chunk_rows(c)] = joined
            stage[level + 1, chunk_rows(c)] = joined.astype(BF16)
            relay_copy(level + 1, c).start()
        else:
            pre_bf[chunk_rows(c)] = fresh.astype(BF16)

    def join_norm(level):
        here, own, other = links[level]
        norm_copy(level).wait_recv()
        got = relay_n[level]
        fresh = here * got
        if level > 0:
            fresh = pre_n[...] + fresh
        pre_n[...] = fresh
        if level < levels - 1:
            joined = own * tot_n[...] + other * got
            tot_n[...] = joined
            stage_n[level + 1] = joined
            norm_copy(level + 1).start()

    def join_due(step):
        for level in range(levels):
            if 0 <= step - 1 - level < nc:
                join(level, step - 1 - level)

    def query_tile(i):
        num[tile(i)] = jnp.zeros((B, C), F32)
        qn[tile(i)] = jnp.zeros((B, 128), F32)

        def key_tile(j, inner):
            scores = lax.dot_general(
                q_all[tile(i)], k_all[tile(j)], (((1,), (1,)), ((), ())), preferred_element_type=F32
            )
            row = rows[j]
            allowed = (i * B + row_i >= j * B + col_i) & (seg_col[tile(i), 0:1] == row[2:3, :])
            exponent = jnp.where(allowed, cum_col[tile(i), 0:1] + row[1:2, :], NONE)
            weighted = jnp.exp(exponent) * (scores * scale)
            qn[tile(i)] += jnp.broadcast_to(jnp.sum(weighted, axis=1, keepdims=True), (B, 128))
            num[tile(i)] += jnp.dot(weighted.astype(BF16), v_all[tile(j)], preferred_element_type=F32)
            return inner

        lax.fori_loop(0, i + 1, key_tile, 0)

    def take_query(d):
        arrive(q_all, q_recv, q_send, source_block(d))
        for g in range(1, group):
            forward(q_all, q_fwd, q_recv, d, g).start()

    def take_others(d):
        for g in range(1, group):
            b = lax.rem(h + heads - d, heads) * group + lax.rem(m + g, group)
            arrive(q_all, q_recv, q_send, b)

    own_key.wait()
    for c in range(nc):
        for d in range(1, heads):
            key_arrive(source_block(d), c)
            for g in range(1, group):
                key_forward(d, g, c).start()
        next_piece()
        for g in range(1, group):
            for hh in range(heads):
                key_arrive(hh * group + lax.rem(m + g, group), c)
        make_state(c)
        join_due(c)
    while queue:
        next_piece()
    tot_n[...] = jnp.zeros_like(tot_n)

    def add_norm(b, carry):
        tail = jnp.broadcast_to(rows[b][3:4, :], (16, B))
        line = lax.broadcasted_iota(jnp.int32, (16, B), 0)
        high = tail.astype(BF16).astype(F32)
        two = jnp.where(line == 0, high, jnp.where(line == 1, tail - high, 0.0)).astype(BF16)
        part = jnp.dot(two, k_all[tile(b)], preferred_element_type=F32)
        tot_n[...] += jnp.broadcast_to(part[0:1] + part[1:2], tot_n.shape)
        return carry

    lax.fori_loop(0, nb, add_norm, 0)
    stage_n[0] = tot_n[...]
    norm_copy(0).start()


    own_copy(q_ref, q_all, q_recv).wait()
    take_others(0)
    query_tile(h)
    join_due(nc)
    join_norm(0)
    take_query(1)
    take_others(1)
    query_tile(lax.rem(h + heads - 1, heads))
    for step in range(nc + 1, nc + levels):
        join_due(step)
    for level in range(1, levels):
        join_norm(level)

    line = lax.broadcasted_iota(jnp.int32, (16, D), 0)
    norm_row = jnp.broadcast_to(pre_n[0:1, :], (16, D))
    norm_high = norm_row.astype(BF16).astype(F32)
    norm_two = jnp.where(
        line == 0, norm_high, jnp.where(line == 1, norm_row - norm_high, 0.0)
    ).astype(BF16)

    def out_copy(b):
        return send(hid.at[block(b)], out_rx.at[t], o_send.at[b], o_recv.at[t], "tensor", b)

    def own_out():
        return pltpu.make_async_copy(hid.at[block(t)], out_rx.at[t], o_recv.at[t])

    def finish_tile(d):
        i = lax.rem(h + heads - d, heads)
        query = q_all[tile(i)]
        entry = jnp.where(
            seg_col[tile(i), 0:1] == first_seg, jnp.exp(cum_col[tile(i), 0:1]), 0.0
        )
        carried = jnp.dot(query, pre_bf[...], preferred_element_type=F32)
        carried_n = jnp.sum(
            lax.dot_general(query, norm_two, (((1,), (1,)), ((), ())), preferred_element_type=F32),
            axis=1,
            keepdims=True,
        )
        bottom = qn[tile(i), 0:1] + entry * carried_n
        top = num[tile(i)] + entry * carried
        hid[tile(i)] = (top / jnp.maximum(jnp.abs(bottom), 1.0)).astype(BF16)
        for g in range(1, group):
            out_copy(i * group + lax.rem(m + g, group)).start()
        if d == 0:
            own_out().start()
        else:
            out_copy(i * group + m).start()

    finish_tile(1)
    finish_tile(0)
    for d in range(2, heads):
        take_query(d)
        take_others(d)
        query_tile(lax.rem(h + heads - d, heads))
        finish_tile(d)

    og_copy.wait()
    own_out().wait()

    def finish_head(step, carry):
        hh = lax.rem(h + step, heads)
        parts = []
        for g in range(group):
            b = hh * group + g

            @pl.when(b != t)
            def _():
                send(
                    hid.at[block(b)], out_rx.at[b], o_send.at[b], o_recv.at[b], "tensor", lax.rem(t + 1, ten_n)
                ).wait_recv()

            parts.append(out_rx[b].astype(F32))
        mean = sum(jnp.sum(x, axis=1, keepdims=True) for x in parts) * (1.0 / D)
        parts = [x - mean for x in parts]
        var = sum(jnp.sum(x * x, axis=1, keepdims=True) for x in parts) * (1.0 / D)
        inv = lax.rsqrt(var + EPS)
        for g in range(group):
            cols = val_cols(hh * group + g)
            gate = og_v[:, cols].astype(F32)
            silu = gate / (1.0 + jnp.exp(-gate))
            out_ref[:, cols] = (parts[g] * inv * gain_ref[:, cols] * silu).astype(BF16)
        return carry

    lax.fori_loop(0, heads, finish_head, 0)

    for d in range(1, ten_n):
        gate_copy(d).wait_send()
        val_copy(d).wait_send()
        out_copy(lax.rem(t + d, ten_n)).wait_send()
    for d in range(1, heads):
        head_copy(q_ref, q_all, q_send, q_recv, d).wait_send()
        for c in range(nc):
            key_copy(d, c).wait_send()
    for g in range(1, group):
        own_forward(q_ref, q_all, q_fwd, q_recv, g).wait_send()
        for c in range(nc):
            for d in range(heads):
                key_forward(d, g, c).wait_send()
        for d in range(1, heads):
            forward(q_all, q_fwd, q_recv, d, g).wait_send()
    for d in range(1, seq_n):
        meta_copy(d).wait_send()
    for level in range(levels):
        norm_copy(level).wait_send()
        for c in range(nc):
            relay_copy(level, c).wait_send()


def on_device(
    seq_n, ten_n, queries, key_rows, values, input_gate, forget_gate, segment_ids, output_gate, norm_gain
):
    R, inner = queries.shape
    heads = input_gate.shape[1]
    D = inner // heads
    group = ten_n // heads
    C = D // group
    N = ten_n * R
    nc = D // min(256, D)
    levels = seq_n.bit_length() - 1
    gates = jnp.concatenate([input_gate, forget_gate], axis=1).astype(F32).T
    lanes = max(R, 128)
    gates = jnp.pad(gates, ((0, -(2 * heads) % 8), (0, lanes - R)))
    lines = gates.shape[0]
    segs = segment_ids.reshape(1, N)
    dma = pltpu.SemaphoreType.DMA
    vmem = pltpu.VMEM
    whole = pl.BlockSpec(memory_space=pltpu.VMEM)
    far = pl.BlockSpec(memory_space=pltpu.HBM)
    forwards = max(1, heads * (group - 1))
    return pl.pallas_call(
        functools.partial(kernel, (seq_n, ten_n, heads, R, D)),
        out_shape=jax.ShapeDtypeStruct((R, inner), BF16),
        in_specs=[whole, whole, whole, far, far, far, far],
        out_specs=whole,
        scratch_shapes=[
            vmem((ten_n, lines, lanes), F32),
            vmem((N, D), BF16),
            vmem((N, C), BF16),
            vmem((N, D), BF16),
            vmem((N, C), BF16),
            vmem((N, 128), F32),
            vmem((N, 128), F32),
            vmem((N, 128), F32),
            vmem((N, 128), F32),
            vmem((N, 128), F32),
            vmem((heads, 8, group * R), F32),
            vmem((8, 128), F32),
            vmem((seq_n, 8, 128), F32),
            vmem((D, C), F32),
            vmem((D, C), F32),
            vmem((D, C), BF16),
            vmem((levels, D, C), BF16),
            vmem((levels, D, C), BF16),
            vmem((8, D), F32),
            vmem((8, D), F32),
            vmem((levels, 8, D), F32),
            vmem((levels, 8, D), F32),
            vmem((N, C), F32),
            vmem((N, 128), F32),
            vmem((N, C), BF16),
            vmem((ten_n, R, C), BF16),
            vmem((R, inner), BF16),
            dma((ten_n,)),
            dma((ten_n,)),
            dma((heads, nc)),
            dma((forwards, nc)),
            dma((ten_n, nc)),
            dma((ten_n,)),
            dma((ten_n,)),
            dma((heads,)),
            dma((forwards,)),
            dma((ten_n,)),
            dma((seq_n,)),
            dma((seq_n,)),
            dma((levels, nc)),
            dma((levels, nc)),
            dma((levels,)),
            dma((levels,)),
            dma((ten_n,)),
            dma((ten_n,)),
            dma,
            dma,
        ],
        compiler_params=pltpu.CompilerParams(
            collective_id=0, has_side_effects=True, vmem_limit_bytes=48 * 1024 * 1024
        ),
        cost_estimate=pl.CostEstimate(
            flops=2 * N * (N * D + N * C + 2 * D * C), bytes_accessed=10 * R * inner, transcendentals=N * N
        ),
    )(gates, segs, norm_gain.reshape(1, inner), queries, key_rows, values, output_gate)


def solution(mesh):
    rows = P(("seq", "tensor"), None)
    return jax.shard_map(
        functools.partial(on_device, mesh.shape["seq"], mesh.shape["tensor"]),
        mesh=mesh,
        in_specs=(rows, rows, rows, rows, rows, P("seq"), rows, P()),
        out_specs=rows,
        check_vma=False,
    )
```

```python
import functools
import math

import jax
import jax.numpy as jnp
from jax import lax
from jax.experimental import pallas as pl
from jax.experimental.pallas import tpu as pltpu
from jax.sharding import PartitionSpec as P

MESH = pl.DeviceIdType.MESH
F32 = jnp.float32
BF16 = jnp.bfloat16
EPS = 1e-05
LIMIT = 63 * 1024 * 1024
NONE = -1e30


def send(src, dst, send_sem, recv_sem, axis, index):
    return pltpu.make_async_remote_copy(
        src_ref=src,
        dst_ref=dst,
        send_sem=send_sem,
        recv_sem=recv_sem,
        device_id={axis: index},
        device_id_type=MESH,
    )


def kernel(
    dims,
    in_gate_ref,
    forget_ref,
    seg_ref,
    gain_ref,
    q_ref,
    k_ref,
    v_ref,
    og_ref,
    out_ref,
    gates_ref,
    gates_all,
    k_all,
    v_all,
    q_all,
    vt,
    lf_col,
    gate_col,
    cum_col,
    seg_col,
    tail_col,
    rows,
    meta,
    meta_all,
    tot,
    pre,
    pre_bf,
    stage,
    relay,
    tot_n,
    pre_n,
    stage_n,
    relay_n,
    num,
    qn,
    hid,
    out_rx,
    og_v,
    g_send,
    g_recv,
    k_send,
    k_fwd,
    k_recv,
    v_send,
    v_recv,
    q_send,
    q_fwd,
    q_recv,
    m_send,
    m_recv,
    r_send,
    r_recv,
    n_send,
    n_recv,
    o_send,
    o_recv,
    og_sem,
    k_own,
    out_v,
    w_sem,
):
    seq_n, ten_n, heads, R, D = dims
    group = ten_n // heads
    C = D // group
    N = ten_n * R
    B = group * R
    nb = heads
    chunk = min(256, D)
    nc = D // chunk
    levels = seq_n.bit_length() - 1
    scale = 1.0 / math.sqrt(D)
    t = lax.axis_index("tensor")
    s = lax.axis_index("seq")
    h = lax.div(t, group)
    m = lax.rem(t, group)

    def block(index):
        return pl.ds(pl.multiple_of(index * R, R), R)

    def tile(index):
        return pl.ds(pl.multiple_of(index * B, B), B)

    def head_cols(index):
        return pl.ds(pl.multiple_of(index * D, 128), D)

    def val_cols(index):
        return pl.ds(pl.multiple_of(index * C, 128), C)

    gates_ref[0:heads, 0:R] = in_gate_ref[...].astype(F32)
    gates_ref[heads : 2 * heads, 0:R] = forget_ref[...].astype(F32)
    barrier = pltpu.get_barrier_semaphore()
    for d in range(1, ten_n):
        pl.semaphore_signal(
            barrier, inc=1, device_id={"tensor": lax.rem(t + d, ten_n)}, device_id_type=MESH
        )
    for d in range(1, seq_n):
        pl.semaphore_signal(
            barrier, inc=1, device_id={"seq": lax.rem(s + d, seq_n)}, device_id_type=MESH
        )
    pl.semaphore_wait(barrier, ten_n + seq_n - 2)

    def gate_copy(d):
        return send(
            gates_ref, gates_all.at[t], g_send.at[d - 1], g_recv.at[t], "tensor", lax.rem(t + d, ten_n)
        )

    def head_copy(src, dst, sem, rsem, d):
        hh = lax.rem(h + d, heads)
        return send(
            src.at[:, head_cols(hh)], dst.at[block(t)], sem.at[d - 1], rsem.at[t], "tensor", hh * group + m
        )

    def own_copy(src, dst, rsem):
        return pltpu.make_async_copy(src.at[:, head_cols(h)], dst.at[block(t)], rsem.at[t])

    def own_forward(src, dst, sem, rsem, g):
        return send(
            src.at[:, head_cols(h)],
            dst.at[block(t)],
            sem.at[g - 1],
            rsem.at[t],
            "tensor",
            h * group + lax.rem(m + g, group),
        )

    def source_block(d):
        return lax.rem(h + heads - d, heads) * group + m

    def forward(dst, sem, rsem, d, g):
        b = source_block(d)
        return send(
            dst.at[block(b)],
            dst.at[block(b)],
            sem.at[d * (group - 1) + g - 1],
            rsem.at[b],
            "tensor",
            h * group + lax.rem(m + g, group),
        )

    def arrive(dst, rsem, sem, b):
        send(dst.at[block(b)], dst.at[block(b)], sem.at[0], rsem.at[b], "tensor", lax.rem(t + 1, ten_n)).wait_recv()

    def key_copy(d, c):
        hh = lax.rem(h + d, heads)
        return send(
            k_ref.at[:, pl.ds(pl.multiple_of(hh * D + c * chunk, 128), chunk)],
            k_all.at[block(t), pl.ds(c * chunk, chunk)],
            k_send.at[d - 1, c],
            k_recv.at[t, c],
            "tensor",
            hh * group + m,
        )

    def key_forward(d, g, c):
        b = source_block(d)
        here = k_all.at[block(b), pl.ds(c * chunk, chunk)]
        source = k_ref.at[:, pl.ds(pl.multiple_of(h * D + c * chunk, 128), chunk)] if d == 0 else here
        return send(
            source,
            here,
            k_fwd.at[d * (group - 1) + g - 1, c],
            k_recv.at[b, c],
            "tensor",
            h * group + lax.rem(m + g, group),
        )

    def key_arrive(b, c):
        here = k_all.at[block(b), pl.ds(c * chunk, chunk)]
        send(here, here, k_send.at[0, c], k_recv.at[b, c], "tensor", lax.rem(t + 1, ten_n)).wait_recv()

    def send_keys(c):
        for d in range(1, heads):
            key_copy(d, c).start()

    def send_queries(d):
        head_copy(q_ref, q_all, q_send, q_recv, d).start()

    def val_copy(d):
        tt = lax.rem(t + d, ten_n)
        return send(
            v_ref.at[:, val_cols(tt)], v_all.at[block(t)], v_send.at[d - 1], v_recv.at[t], "tensor", tt
        )

    for d in range(1, ten_n):
        gate_copy(d).start()
    gates_all[t] = gates_ref[...]
    for d in range(1, ten_n):
        val_copy(d).start()
    own_val = pltpu.make_async_copy(v_ref.at[:, val_cols(t)], v_all.at[block(t)], v_recv.at[t])
    own_val.start()
    own_key = pltpu.make_async_copy(k_ref.at[:, head_cols(h)], k_all.at[block(t)], k_own)
    own_key.start()
    own_copy(q_ref, q_all, q_recv).start()
    for g in range(1, group):
        for c in range(nc):
            key_forward(0, g, c).start()
        own_forward(q_ref, q_all, q_fwd, q_recv, g).start()
    queue = [functools.partial(send_keys, c) for c in range(nc)]
    queue += [functools.partial(send_queries, d) for d in range(1, heads)]

    def next_piece():
        if queue:
            queue.pop(0)()

    next_piece()
    next_piece()
    og_copy = pltpu.make_async_copy(og_ref, og_v, og_sem)
    og_copy.start()

    for d in range(1, ten_n):
        b = lax.rem(t + ten_n - d, ten_n)
        send(
            gates_ref, gates_all.at[b], g_send.at[0], g_recv.at[b], "tensor", lax.rem(t + 1, ten_n)
        ).wait_recv()
    eye_r = lax.broadcasted_iota(jnp.int32, (R, R), 0) == lax.broadcasted_iota(jnp.int32, (R, R), 1)

    def spread_gates(b, carry):
        both = gates_all[b]
        line = lax.broadcasted_iota(jnp.int32, both.shape, 0)
        gate_in = jnp.sum(jnp.where(line == h, both, 0.0), axis=0, keepdims=True)[:, :R]
        pre_f = jnp.sum(jnp.where(line == h + heads, both, 0.0), axis=0, keepdims=True)[:, :R]
        log_f = jnp.minimum(pre_f, 0.0) - jnp.log1p(jnp.exp(-jnp.abs(pre_f)))
        to_col = lambda row: jnp.broadcast_to(
            jnp.sum(jnp.where(eye_r, jnp.broadcast_to(row, (R, R)), 0.0), axis=1, keepdims=True), (R, 128)
        )
        lf_col[block(b)] = to_col(log_f)
        gate_col[block(b)] = to_col(gate_in)
        return carry

    lax.fori_loop(0, ten_n, spread_gates, 0)
    row_i = lax.broadcasted_iota(jnp.int32, (B, B), 0)
    col_i = lax.broadcasted_iota(jnp.int32, (B, B), 1)
    eye = row_i == col_i

    def as_row(mask, col):
        return jnp.sum(jnp.where(mask, jnp.broadcast_to(col, (B, B)), 0.0), axis=0, keepdims=True)

    def as_col(row):
        return jnp.broadcast_to(
            jnp.sum(jnp.where(eye, jnp.broadcast_to(row, (B, B)), 0.0), axis=1, keepdims=True), (B, 128)
        )

    def segs(b):
        return seg_ref[0:1, b * B : (b + 1) * B].astype(F32)

    total = jnp.zeros((1, 1), F32)
    for b in range(nb):
        here = pl.ds(b * B, B)
        cum = as_row(row_i <= col_i, lf_col[here, 0:1]) + total
        total = cum[:, B - 1 : B]
        rows[b, 0:1, :] = cum
        rows[b, 1:2, :] = as_row(eye, gate_col[here, 0:1]) - cum
        rows[b, 2:3, :] = segs(b)
        cum_col[here] = as_col(cum)
        seg_col[here] = as_col(segs(b))
    first_seg = segs(0)[:, 0:1]
    last_seg = segs(nb - 1)[:, B - 1 : B]
    for b in range(nb):
        here = pl.ds(b * B, B)
        kept = rows[b, 2:3, :] == last_seg
        tail = jnp.where(kept, jnp.exp(total + rows[b, 1:2, :]) * scale, 0.0)
        rows[b, 3:4, :] = tail
        tail_col[here] = as_col(tail)
    meta[0:1, :] = jnp.broadcast_to(total, (1, 128))
    meta[1:2, :] = jnp.broadcast_to(first_seg, (1, 128))
    meta[2:8, :] = jnp.broadcast_to(last_seg, (6, 128))

    def meta_copy(d):
        return send(
            meta, meta_all.at[s], m_send.at[d - 1], m_recv.at[s], "seq", lax.rem(s + d, seq_n)
        )

    for d in range(1, seq_n):
        meta_copy(d).start()
    meta_all[s] = meta[...]

    for d in range(1, ten_n):
        arrive(v_all, v_recv, v_send, lax.rem(t + ten_n - d, ten_n))
    own_val.wait()
    next_piece()

    def scale_values(b, carry):
        vt[tile(b)] = (v_all[tile(b)].astype(F32) * tail_col[tile(b), 0:1]).astype(BF16)
        return carry

    lax.fori_loop(0, nb, scale_values, 0)
    def chunk_rows(c):
        return pl.ds(pl.multiple_of(c * chunk, chunk), chunk)

    def relay_copy(level, c):
        return send(
            stage.at[level, chunk_rows(c)],
            relay.at[level, chunk_rows(c)],
            r_send.at[level, c],
            r_recv.at[level, c],
            "seq",
            s + (1 - 2 * lax.rem(lax.div(s, 1 << level), 2)) * (1 << level),
        )

    def norm_copy(level):
        return send(
            stage_n.at[level],
            relay_n.at[level],
            n_send.at[level],
            n_recv.at[level],
            "seq",
            s + (1 - 2 * lax.rem(lax.div(s, 1 << level), 2)) * (1 << level),
        )

    def make_state(c):
        part = lax.dot_general(
            k_all[:, pl.ds(c * chunk, chunk)], vt[...], (((0,), (0,)), ((), ())), preferred_element_type=F32
        )
        tot[chunk_rows(c)] = part
        stage[0, chunk_rows(c)] = part.astype(BF16)
        relay_copy(0, c).start()

    for d in range(1, seq_n):
        b = lax.rem(s + seq_n - d, seq_n)
        send(
            meta, meta_all.at[b], m_send.at[0], m_recv.at[b], "seq", lax.rem(s + 1, seq_n)
        ).wait_recv()

    def factors(level):
        width = 1 << level
        upper = lax.rem(lax.div(s, width), 2)
        base = lax.div(s, 2 * width) * (2 * width)
        low_end = base + width - 1
        high_end = base + 2 * width - 1
        to_here = jnp.zeros((1, 128), F32)
        to_end = jnp.zeros((1, 128), F32)
        for u in range(seq_n):
            log_u = meta_all[u][0:1, :]
            to_here = to_here + jnp.where((u > low_end) & (u < s), log_u, 0.0)
            to_end = to_end + jnp.where((u > low_end) & (u <= high_end), log_u, 0.0)
        low_last = meta_all[low_end][2:3, :]
        here = jnp.where(low_last == first_seg, jnp.exp(to_here), 0.0)
        end = jnp.where(low_last == meta_all[high_end][2:3, :], jnp.exp(to_end), 0.0)
        here = jnp.where(upper == 1, here, 0.0)[:, 0:1]
        own = jnp.where(upper == 1, 1.0, end)[:, 0:1]
        other = jnp.where(upper == 1, end, 1.0)[:, 0:1]
        return here, own, other

    links = [factors(level) for level in range(levels)]

    def join(level, c):
        here, own, other = links[level]
        relay_copy(level, c).wait_recv()
        got = relay[level, chunk_rows(c)].astype(F32)
        fresh = here * got
        if level > 0:
            fresh = pre[chunk_rows(c)] + fresh
        if level < levels - 1:
            pre[chunk_rows(c)] = fresh
            joined = own * tot[chunk_rows(c)] + other * got
            tot[chunk_rows(c)] = joined
            stage[level + 1, chunk_rows(c)] = joined.astype(BF16)
            relay_copy(level + 1, c).start()
        else:
            pre_bf[chunk_rows(c)] = fresh.astype(BF16)

    def join_norm(level):
        here, own, other = links[level]
        norm_copy(level).wait_recv()
        got = relay_n[level]
        fresh = here * got
        if level > 0:
            fresh = pre_n[...] + fresh
        pre_n[...] = fresh
        if level < levels - 1:
            joined = own * tot_n[...] + other * got
            tot_n[...] = joined
            stage_n[level + 1] = joined
            norm_copy(level + 1).start()

    def join_due(step):
        for level in range(levels):
            if 0 <= step - 1 - level < nc:
                join(level, step - 1 - level)

    def query_tile(i):
        num[tile(i)] = jnp.zeros((B, C), F32)
        qn[tile(i)] = jnp.zeros((B, 128), F32)

        def key_tile(j, inner):
            scores = lax.dot_general(
                q_all[tile(i)], k_all[tile(j)], (((1,), (1,)), ((), ())), preferred_element_type=F32
            )
            row = rows[j]
            allowed = (i * B + row_i >= j * B + col_i) & (seg_col[tile(i), 0:1] == row[2:3, :])
            exponent = jnp.where(allowed, cum_col[tile(i), 0:1] + row[1:2, :], NONE)
            weighted = jnp.exp(exponent) * (scores * scale)
            qn[tile(i)] += jnp.broadcast_to(jnp.sum(weighted, axis=1, keepdims=True), (B, 128))
            num[tile(i)] += jnp.dot(weighted.astype(BF16), v_all[tile(j)], preferred_element_type=F32)
            return inner

        lax.fori_loop(0, i + 1, key_tile, 0)

    def take_query(d):
        arrive(q_all, q_recv, q_send, source_block(d))
        for g in range(1, group):
            forward(q_all, q_fwd, q_recv, d, g).start()

    def take_others(d):
        for g in range(1, group):
            b = lax.rem(h + heads - d, heads) * group + lax.rem(m + g, group)
            arrive(q_all, q_recv, q_send, b)

    own_key.wait()
    for c in range(nc):
        for d in range(1, heads):
            key_arrive(source_block(d), c)
            for g in range(1, group):
                key_forward(d, g, c).start()
        next_piece()
        for g in range(1, group):
            for hh in range(heads):
                key_arrive(hh * group + lax.rem(m + g, group), c)
        make_state(c)
        join_due(c)
    while queue:
        next_piece()
    tot_n[...] = jnp.zeros_like(tot_n)

    def add_norm(b, carry):
        tail = jnp.broadcast_to(rows[b][3:4, :], (16, B))
        line = lax.broadcasted_iota(jnp.int32, (16, B), 0)
        high = tail.astype(BF16).astype(F32)
        two = jnp.where(line == 0, high, jnp.where(line == 1, tail - high, 0.0)).astype(BF16)
        part = jnp.dot(two, k_all[tile(b)], preferred_element_type=F32)
        tot_n[...] += jnp.broadcast_to(part[0:1] + part[1:2], tot_n.shape)
        return carry

    lax.fori_loop(0, nb, add_norm, 0)
    stage_n[0] = tot_n[...]
    norm_copy(0).start()


    own_copy(q_ref, q_all, q_recv).wait()
    take_others(0)
    query_tile(h)
    join_due(nc)
    join_norm(0)
    take_query(1)
    take_others(1)
    query_tile(lax.rem(h + heads - 1, heads))
    for step in range(nc + 1, nc + levels):
        join_due(step)
    for level in range(1, levels):
        join_norm(level)

    line = lax.broadcasted_iota(jnp.int32, (16, D), 0)
    norm_row = jnp.broadcast_to(pre_n[0:1, :], (16, D))
    norm_high = norm_row.astype(BF16).astype(F32)
    norm_two = jnp.where(
        line == 0, norm_high, jnp.where(line == 1, norm_row - norm_high, 0.0)
    ).astype(BF16)

    def out_copy(b):
        return send(hid.at[block(b)], out_rx.at[t], o_send.at[b], o_recv.at[t], "tensor", b)

    def own_out():
        return pltpu.make_async_copy(hid.at[block(t)], out_rx.at[t], o_recv.at[t])

    def finish_tile(d):
        i = lax.rem(h + heads - d, heads)
        query = q_all[tile(i)]
        entry = jnp.where(
            seg_col[tile(i), 0:1] == first_seg, jnp.exp(cum_col[tile(i), 0:1]), 0.0
        )
        carried = jnp.dot(query, pre_bf[...], preferred_element_type=F32)
        carried_n = jnp.sum(
            lax.dot_general(query, norm_two, (((1,), (1,)), ((), ())), preferred_element_type=F32),
            axis=1,
            keepdims=True,
        )
        bottom = qn[tile(i), 0:1] + entry * carried_n
        top = num[tile(i)] + entry * carried
        hid[tile(i)] = (top / jnp.maximum(jnp.abs(bottom), 1.0)).astype(BF16)
        for g in range(1, group):
            out_copy(i * group + lax.rem(m + g, group)).start()
        if d == 0:
            own_out().start()
        else:
            out_copy(i * group + m).start()

    finish_tile(1)
    finish_tile(0)
    for d in range(2, heads):
        take_query(d)
        take_others(d)
        query_tile(lax.rem(h + heads - d, heads))
        finish_tile(d)

    og_copy.wait()
    own_out().wait()

    def write_copy(hh):
        return pltpu.make_async_copy(
            out_v.at[:, head_cols(hh)], out_ref.at[:, head_cols(hh)], w_sem.at[hh]
        )

    def finish_head(step, carry):
        hh = lax.rem(h + step, heads)
        parts = []
        for g in range(group):
            b = hh * group + g

            @pl.when(b != t)
            def _():
                send(
                    hid.at[block(b)], out_rx.at[b], o_send.at[b], o_recv.at[b], "tensor", lax.rem(t + 1, ten_n)
                ).wait_recv()

            parts.append(out_rx[b].astype(F32))
        mean = sum(jnp.sum(x, axis=1, keepdims=True) for x in parts) * (1.0 / D)
        parts = [x - mean for x in parts]
        var = sum(jnp.sum(x * x, axis=1, keepdims=True) for x in parts) * (1.0 / D)
        inv = lax.rsqrt(var + EPS)
        for g in range(group):
            cols = val_cols(hh * group + g)
            gate = og_v[:, cols].astype(F32)
            silu = gate / (1.0 + jnp.exp(-gate))
            out_v[:, cols] = (parts[g] * inv * gain_ref[:, cols] * silu).astype(BF16)
        write_copy(hh).start()
        return carry

    lax.fori_loop(0, heads, finish_head, 0)

    for d in range(1, ten_n):
        gate_copy(d).wait_send()
        val_copy(d).wait_send()
        out_copy(lax.rem(t + d, ten_n)).wait_send()
    for d in range(1, heads):
        head_copy(q_ref, q_all, q_send, q_recv, d).wait_send()
        for c in range(nc):
            key_copy(d, c).wait_send()
    for g in range(1, group):
        own_forward(q_ref, q_all, q_fwd, q_recv, g).wait_send()
        for c in range(nc):
            for d in range(heads):
                key_forward(d, g, c).wait_send()
        for d in range(1, heads):
            forward(q_all, q_fwd, q_recv, d, g).wait_send()
    for d in range(1, seq_n):
        meta_copy(d).wait_send()
    for hh in range(heads):
        write_copy(hh).wait()
    for level in range(levels):
        norm_copy(level).wait_send()
        for c in range(nc):
            relay_copy(level, c).wait_send()


def on_device(
    seq_n, ten_n, queries, key_rows, values, input_gate, forget_gate, segment_ids, output_gate, norm_gain
):
    R, inner = queries.shape
    heads = input_gate.shape[1]
    D = inner // heads
    group = ten_n // heads
    C = D // group
    N = ten_n * R
    nc = D // min(256, D)
    levels = seq_n.bit_length() - 1
    lanes = max(R, 128)
    lines = 2 * heads
    segs = segment_ids.reshape(1, N)
    dma = pltpu.SemaphoreType.DMA
    vmem = pltpu.VMEM
    whole = pl.BlockSpec(memory_space=pltpu.VMEM)
    far = pl.BlockSpec(memory_space=pltpu.HBM)
    forwards = max(1, heads * (group - 1))
    return pl.pallas_call(
        functools.partial(kernel, (seq_n, ten_n, heads, R, D)),
        out_shape=jax.ShapeDtypeStruct((R, inner), BF16),
        in_specs=[whole, whole, whole, whole, far, far, far, far],
        out_specs=far,
        scratch_shapes=[
            vmem((lines, lanes), F32),
            vmem((ten_n, lines, lanes), F32),
            vmem((N, D), BF16),
            vmem((N, C), BF16),
            vmem((N, D), BF16),
            vmem((N, C), BF16),
            vmem((N, 128), F32),
            vmem((N, 128), F32),
            vmem((N, 128), F32),
            vmem((N, 128), F32),
            vmem((N, 128), F32),
            vmem((heads, 8, group * R), F32),
            vmem((8, 128), F32),
            vmem((seq_n, 8, 128), F32),
            vmem((D, C), F32),
            vmem((D, C), F32),
            vmem((D, C), BF16),
            vmem((levels, D, C), BF16),
            vmem((levels, D, C), BF16),
            vmem((8, D), F32),
            vmem((8, D), F32),
            vmem((levels, 8, D), F32),
            vmem((levels, 8, D), F32),
            vmem((N, C), F32),
            vmem((N, 128), F32),
            vmem((N, C), BF16),
            vmem((ten_n, R, C), BF16),
            vmem((R, inner), BF16),
            dma((ten_n,)),
            dma((ten_n,)),
            dma((heads, nc)),
            dma((forwards, nc)),
            dma((ten_n, nc)),
            dma((ten_n,)),
            dma((ten_n,)),
            dma((heads,)),
            dma((forwards,)),
            dma((ten_n,)),
            dma((seq_n,)),
            dma((seq_n,)),
            dma((levels, nc)),
            dma((levels, nc)),
            dma((levels,)),
            dma((levels,)),
            dma((ten_n,)),
            dma((ten_n,)),
            dma,
            dma,
            vmem((R, inner), BF16),
            dma((heads,)),
        ],
        compiler_params=pltpu.CompilerParams(
            collective_id=0, has_side_effects=True, vmem_limit_bytes=LIMIT
        ),
        cost_estimate=pl.CostEstimate(
            flops=2 * N * (N * D + N * C + 2 * D * C), bytes_accessed=10 * R * inner, transcendentals=N * N
        ),
    )(input_gate.T, forget_gate.T, segs, norm_gain.reshape(1, inner), queries, key_rows, values, output_gate)


def solution(mesh):
    rows = P(("seq", "tensor"), None)
    return jax.shard_map(
        functools.partial(on_device, mesh.shape["seq"], mesh.shape["tensor"]),
        mesh=mesh,
        in_specs=(rows, rows, rows, rows, rows, P("seq"), rows, P()),
        out_specs=rows,
        check_vma=False,
    )
```

```python
import functools
import math

import jax
import jax.numpy as jnp
from jax import lax
from jax.experimental import pallas as pl
from jax.experimental.pallas import tpu as pltpu
from jax.sharding import PartitionSpec as P

MESH = pl.DeviceIdType.MESH
F32 = jnp.float32
BF16 = jnp.bfloat16
EPS = 1e-05
LIMIT = 62 * 1024 * 1024 + 512 * 1024
NONE = -1e30


def send(src, dst, send_sem, recv_sem, axis, index):
    return pltpu.make_async_remote_copy(
        src_ref=src,
        dst_ref=dst,
        send_sem=send_sem,
        recv_sem=recv_sem,
        device_id={axis: index},
        device_id_type=MESH,
    )


def kernel(
    dims,
    in_gate_ref,
    forget_ref,
    seg_hbm,
    gain_hbm,
    q_ref,
    k_ref,
    v_ref,
    og_ref,
    out_ref,
    gates_ref,
    gates_all,
    k_all,
    v_all,
    q_all,
    vt,
    lf_col,
    gate_col,
    cum_col,
    seg_col,
    tail_col,
    rows,
    meta,
    meta_all,
    tot,
    pre,
    pre_bf,
    stage,
    relay,
    tot_n,
    pre_n,
    stage_n,
    relay_n,
    num,
    qn,
    hid,
    out_rx,
    og_v,
    g_send,
    g_recv,
    k_send,
    k_fwd,
    k_recv,
    v_send,
    v_recv,
    q_send,
    q_fwd,
    q_recv,
    m_send,
    m_recv,
    r_send,
    r_recv,
    n_send,
    n_recv,
    o_send,
    o_recv,
    og_sem,
    k_own,
    out_v,
    w_sem,
    seg_ref,
    gain_ref,
    small_sem,
):
    seq_n, ten_n, heads, R, D = dims
    group = ten_n // heads
    C = D // group
    N = ten_n * R
    B = group * R
    nb = heads
    chunk = min(256, D)
    nc = D // chunk
    levels = seq_n.bit_length() - 1
    scale = 1.0 / math.sqrt(D)
    t = lax.axis_index("tensor")
    s = lax.axis_index("seq")
    h = lax.div(t, group)
    m = lax.rem(t, group)

    def block(index):
        return pl.ds(pl.multiple_of(index * R, R), R)

    def tile(index):
        return pl.ds(pl.multiple_of(index * B, B), B)

    def head_cols(index):
        return pl.ds(pl.multiple_of(index * D, 128), D)

    def val_cols(index):
        return pl.ds(pl.multiple_of(index * C, 128), C)

    small = [
        pltpu.make_async_copy(a, b, small_sem.at[i])
        for i, (a, b) in enumerate([(seg_hbm, seg_ref), (gain_hbm, gain_ref)])
    ]
    for copy in small:
        copy.start()
    barrier = pltpu.get_barrier_semaphore()
    for d in range(1, ten_n):
        pl.semaphore_signal(
            barrier, inc=1, device_id={"tensor": lax.rem(t + d, ten_n)}, device_id_type=MESH
        )
    for d in range(1, seq_n):
        pl.semaphore_signal(
            barrier, inc=1, device_id={"seq": lax.rem(s + d, seq_n)}, device_id_type=MESH
        )
    pl.semaphore_wait(barrier, ten_n + seq_n - 2)

    def gate_copy(d):
        return send(
            gates_ref, gates_all.at[t], g_send.at[d - 1], g_recv.at[t], "tensor", lax.rem(t + d, ten_n)
        )

    def head_copy(src, dst, sem, rsem, d):
        hh = lax.rem(h + d, heads)
        return send(
            src.at[:, head_cols(hh)], dst.at[block(t)], sem.at[d - 1], rsem.at[t], "tensor", hh * group + m
        )

    def own_copy(src, dst, rsem):
        return pltpu.make_async_copy(src.at[:, head_cols(h)], dst.at[block(t)], rsem.at[t])

    def own_forward(src, dst, sem, rsem, g):
        return send(
            src.at[:, head_cols(h)],
            dst.at[block(t)],
            sem.at[g - 1],
            rsem.at[t],
            "tensor",
            h * group + lax.rem(m + g, group),
        )

    def source_block(d):
        return lax.rem(h + heads - d, heads) * group + m

    def forward(dst, sem, rsem, d, g):
        b = source_block(d)
        return send(
            dst.at[block(b)],
            dst.at[block(b)],
            sem.at[d * (group - 1) + g - 1],
            rsem.at[b],
            "tensor",
            h * group + lax.rem(m + g, group),
        )

    def arrive(dst, rsem, sem, b):
        send(dst.at[block(b)], dst.at[block(b)], sem.at[0], rsem.at[b], "tensor", lax.rem(t + 1, ten_n)).wait_recv()

    def key_copy(d, c):
        hh = lax.rem(h + d, heads)
        return send(
            k_ref.at[:, pl.ds(pl.multiple_of(hh * D + c * chunk, 128), chunk)],
            k_all.at[block(t), pl.ds(c * chunk, chunk)],
            k_send.at[d - 1, c],
            k_recv.at[t, c],
            "tensor",
            hh * group + m,
        )

    def key_forward(d, g, c):
        b = source_block(d)
        here = k_all.at[block(b), pl.ds(c * chunk, chunk)]
        source = k_ref.at[:, pl.ds(pl.multiple_of(h * D + c * chunk, 128), chunk)] if d == 0 else here
        return send(
            source,
            here,
            k_fwd.at[d * (group - 1) + g - 1, c],
            k_recv.at[b, c],
            "tensor",
            h * group + lax.rem(m + g, group),
        )

    def key_arrive(b, c):
        here = k_all.at[block(b), pl.ds(c * chunk, chunk)]
        send(here, here, k_send.at[0, c], k_recv.at[b, c], "tensor", lax.rem(t + 1, ten_n)).wait_recv()

    def send_keys(c):
        for d in range(1, heads):
            key_copy(d, c).start()

    def send_queries(d):
        head_copy(q_ref, q_all, q_send, q_recv, d).start()

    def val_copy(d):
        tt = lax.rem(t + d, ten_n)
        return send(
            v_ref.at[:, val_cols(tt)], v_all.at[block(t)], v_send.at[d - 1], v_recv.at[t], "tensor", tt
        )

    for d in range(1, ten_n):
        val_copy(d).start()
    gates_ref[0:heads, 0:R] = in_gate_ref[...].astype(F32)
    gates_ref[heads : 2 * heads, 0:R] = forget_ref[...].astype(F32)
    for d in range(1, ten_n):
        gate_copy(d).start()
    gates_all[t] = gates_ref[...]
    own_val = pltpu.make_async_copy(v_ref.at[:, val_cols(t)], v_all.at[block(t)], v_recv.at[t])
    own_val.start()
    own_key = pltpu.make_async_copy(k_ref.at[:, head_cols(h)], k_all.at[block(t)], k_own)
    own_key.start()
    own_copy(q_ref, q_all, q_recv).start()
    for g in range(1, group):
        for c in range(nc):
            key_forward(0, g, c).start()
        own_forward(q_ref, q_all, q_fwd, q_recv, g).start()
    queue = [functools.partial(send_keys, c) for c in range(nc)]
    queue += [functools.partial(send_queries, d) for d in range(1, heads)]

    def next_piece():
        if queue:
            queue.pop(0)()

    next_piece()
    next_piece()
    og_copy = pltpu.make_async_copy(og_ref, og_v, og_sem)
    og_copy.start()

    for d in range(1, ten_n):
        b = lax.rem(t + ten_n - d, ten_n)
        send(
            gates_ref, gates_all.at[b], g_send.at[0], g_recv.at[b], "tensor", lax.rem(t + 1, ten_n)
        ).wait_recv()
    eye_r = lax.broadcasted_iota(jnp.int32, (R, R), 0) == lax.broadcasted_iota(jnp.int32, (R, R), 1)

    def spread_gates(b, carry):
        both = gates_all[b]
        line = lax.broadcasted_iota(jnp.int32, both.shape, 0)
        gate_in = jnp.sum(jnp.where(line == h, both, 0.0), axis=0, keepdims=True)[:, :R]
        pre_f = jnp.sum(jnp.where(line == h + heads, both, 0.0), axis=0, keepdims=True)[:, :R]
        log_f = jnp.minimum(pre_f, 0.0) - jnp.log1p(jnp.exp(-jnp.abs(pre_f)))
        to_col = lambda row: jnp.broadcast_to(
            jnp.sum(jnp.where(eye_r, jnp.broadcast_to(row, (R, R)), 0.0), axis=1, keepdims=True), (R, 128)
        )
        lf_col[block(b)] = to_col(log_f)
        gate_col[block(b)] = to_col(gate_in)
        return carry

    lax.fori_loop(0, ten_n, spread_gates, 0)
    row_i = lax.broadcasted_iota(jnp.int32, (B, B), 0)
    col_i = lax.broadcasted_iota(jnp.int32, (B, B), 1)
    eye = row_i == col_i

    def as_row(mask, col):
        return jnp.sum(jnp.where(mask, jnp.broadcast_to(col, (B, B)), 0.0), axis=0, keepdims=True)

    def as_col(row):
        return jnp.broadcast_to(
            jnp.sum(jnp.where(eye, jnp.broadcast_to(row, (B, B)), 0.0), axis=1, keepdims=True), (B, 128)
        )

    for copy in small:
        copy.wait()

    def segs(b):
        return seg_ref[0:1, b * B : (b + 1) * B].astype(F32)

    total = jnp.zeros((1, 1), F32)
    for b in range(nb):
        here = pl.ds(b * B, B)
        cum = as_row(row_i <= col_i, lf_col[here, 0:1]) + total
        total = cum[:, B - 1 : B]
        rows[b, 0:1, :] = cum
        rows[b, 1:2, :] = as_row(eye, gate_col[here, 0:1]) - cum
        rows[b, 2:3, :] = segs(b)
        cum_col[here] = as_col(cum)
        seg_col[here] = as_col(segs(b))
    first_seg = segs(0)[:, 0:1]
    last_seg = segs(nb - 1)[:, B - 1 : B]
    for b in range(nb):
        here = pl.ds(b * B, B)
        kept = rows[b, 2:3, :] == last_seg
        tail = jnp.where(kept, jnp.exp(total + rows[b, 1:2, :]) * scale, 0.0)
        rows[b, 3:4, :] = tail
        tail_col[here] = as_col(tail)
    meta[0:1, :] = jnp.broadcast_to(total, (1, 128))
    meta[1:2, :] = jnp.broadcast_to(first_seg, (1, 128))
    meta[2:8, :] = jnp.broadcast_to(last_seg, (6, 128))

    def meta_copy(d):
        return send(
            meta, meta_all.at[s], m_send.at[d - 1], m_recv.at[s], "seq", lax.rem(s + d, seq_n)
        )

    for d in range(1, seq_n):
        meta_copy(d).start()
    meta_all[s] = meta[...]

    for d in range(1, ten_n):
        arrive(v_all, v_recv, v_send, lax.rem(t + ten_n - d, ten_n))
    own_val.wait()
    next_piece()

    def scale_values(b, carry):
        vt[tile(b)] = (v_all[tile(b)].astype(F32) * tail_col[tile(b), 0:1]).astype(BF16)
        return carry

    lax.fori_loop(0, nb, scale_values, 0)
    def chunk_rows(c):
        return pl.ds(pl.multiple_of(c * chunk, chunk), chunk)

    def relay_copy(level, c):
        return send(
            stage.at[level, chunk_rows(c)],
            relay.at[level, chunk_rows(c)],
            r_send.at[level, c],
            r_recv.at[level, c],
            "seq",
            s + (1 - 2 * lax.rem(lax.div(s, 1 << level), 2)) * (1 << level),
        )

    def norm_copy(level):
        return send(
            stage_n.at[level],
            relay_n.at[level],
            n_send.at[level],
            n_recv.at[level],
            "seq",
            s + (1 - 2 * lax.rem(lax.div(s, 1 << level), 2)) * (1 << level),
        )

    def make_state(c):
        part = lax.dot_general(
            k_all[:, pl.ds(c * chunk, chunk)], vt[...], (((0,), (0,)), ((), ())), preferred_element_type=F32
        )
        tot[chunk_rows(c)] = part
        stage[0, chunk_rows(c)] = part.astype(BF16)
        relay_copy(0, c).start()

    for d in range(1, seq_n):
        b = lax.rem(s + seq_n - d, seq_n)
        send(
            meta, meta_all.at[b], m_send.at[0], m_recv.at[b], "seq", lax.rem(s + 1, seq_n)
        ).wait_recv()

    def factors(level):
        width = 1 << level
        upper = lax.rem(lax.div(s, width), 2)
        base = lax.div(s, 2 * width) * (2 * width)
        low_end = base + width - 1
        high_end = base + 2 * width - 1
        to_here = jnp.zeros((1, 128), F32)
        to_end = jnp.zeros((1, 128), F32)
        for u in range(seq_n):
            log_u = meta_all[u][0:1, :]
            to_here = to_here + jnp.where((u > low_end) & (u < s), log_u, 0.0)
            to_end = to_end + jnp.where((u > low_end) & (u <= high_end), log_u, 0.0)
        low_last = meta_all[low_end][2:3, :]
        here = jnp.where(low_last == first_seg, jnp.exp(to_here), 0.0)
        end = jnp.where(low_last == meta_all[high_end][2:3, :], jnp.exp(to_end), 0.0)
        here = jnp.where(upper == 1, here, 0.0)[:, 0:1]
        own = jnp.where(upper == 1, 1.0, end)[:, 0:1]
        other = jnp.where(upper == 1, end, 1.0)[:, 0:1]
        return here, own, other

    links = [factors(level) for level in range(levels)]

    def join(level, c):
        here, own, other = links[level]
        relay_copy(level, c).wait_recv()
        got = relay[level, chunk_rows(c)].astype(F32)
        fresh = here * got
        if level > 0:
            fresh = pre[chunk_rows(c)] + fresh
        if level < levels - 1:
            pre[chunk_rows(c)] = fresh
            joined = own * tot[chunk_rows(c)] + other * got
            tot[chunk_rows(c)] = joined
            stage[level + 1, chunk_rows(c)] = joined.astype(BF16)
            relay_copy(level + 1, c).start()
        else:
            pre_bf[chunk_rows(c)] = fresh.astype(BF16)

    def join_norm(level):
        here, own, other = links[level]
        norm_copy(level).wait_recv()
        got = relay_n[level]
        fresh = here * got
        if level > 0:
            fresh = pre_n[...] + fresh
        pre_n[...] = fresh
        if level < levels - 1:
            joined = own * tot_n[...] + other * got
            tot_n[...] = joined
            stage_n[level + 1] = joined
            norm_copy(level + 1).start()

    def join_due(step):
        for level in range(levels):
            if 0 <= step - 1 - level < nc:
                join(level, step - 1 - level)

    def query_tile(i):
        num[tile(i)] = jnp.zeros((B, C), F32)
        qn[tile(i)] = jnp.zeros((B, 128), F32)

        def key_tile(j, inner):
            scores = lax.dot_general(
                q_all[tile(i)], k_all[tile(j)], (((1,), (1,)), ((), ())), preferred_element_type=F32
            )
            row = rows[j]
            allowed = (i * B + row_i >= j * B + col_i) & (seg_col[tile(i), 0:1] == row[2:3, :])
            exponent = jnp.where(allowed, cum_col[tile(i), 0:1] + row[1:2, :], NONE)
            weighted = jnp.exp(exponent) * (scores * scale)
            qn[tile(i)] += jnp.broadcast_to(jnp.sum(weighted, axis=1, keepdims=True), (B, 128))
            num[tile(i)] += jnp.dot(weighted.astype(BF16), v_all[tile(j)], preferred_element_type=F32)
            return inner

        lax.fori_loop(0, i + 1, key_tile, 0)

    def take_query(d):
        arrive(q_all, q_recv, q_send, source_block(d))
        for g in range(1, group):
            forward(q_all, q_fwd, q_recv, d, g).start()

    def take_others(d):
        for g in range(1, group):
            b = lax.rem(h + heads - d, heads) * group + lax.rem(m + g, group)
            arrive(q_all, q_recv, q_send, b)

    own_key.wait()
    for c in range(nc):
        for d in range(1, heads):
            key_arrive(source_block(d), c)
            for g in range(1, group):
                key_forward(d, g, c).start()
        next_piece()
        for g in range(1, group):
            for hh in range(heads):
                key_arrive(hh * group + lax.rem(m + g, group), c)
        make_state(c)
        join_due(c)
    while queue:
        next_piece()
    tot_n[...] = jnp.zeros_like(tot_n)

    def add_norm(b, carry):
        tail = jnp.broadcast_to(rows[b][3:4, :], (16, B))
        line = lax.broadcasted_iota(jnp.int32, (16, B), 0)
        high = tail.astype(BF16).astype(F32)
        two = jnp.where(line == 0, high, jnp.where(line == 1, tail - high, 0.0)).astype(BF16)
        part = jnp.dot(two, k_all[tile(b)], preferred_element_type=F32)
        tot_n[...] += jnp.broadcast_to(part[0:1] + part[1:2], tot_n.shape)
        return carry

    lax.fori_loop(0, nb, add_norm, 0)
    stage_n[0] = tot_n[...]
    norm_copy(0).start()


    own_copy(q_ref, q_all, q_recv).wait()
    take_others(0)
    query_tile(h)
    join_due(nc)
    join_norm(0)
    take_query(1)
    take_others(1)
    query_tile(lax.rem(h + heads - 1, heads))
    for step in range(nc + 1, nc + levels):
        join_due(step)
    for level in range(1, levels):
        join_norm(level)

    line = lax.broadcasted_iota(jnp.int32, (16, D), 0)
    norm_row = jnp.broadcast_to(pre_n[0:1, :], (16, D))
    norm_high = norm_row.astype(BF16).astype(F32)
    norm_two = jnp.where(
        line == 0, norm_high, jnp.where(line == 1, norm_row - norm_high, 0.0)
    ).astype(BF16)

    def out_copy(b):
        return send(hid.at[block(b)], out_rx.at[t], o_send.at[b], o_recv.at[t], "tensor", b)

    def own_out():
        return pltpu.make_async_copy(hid.at[block(t)], out_rx.at[t], o_recv.at[t])

    def finish_tile(d):
        i = lax.rem(h + heads - d, heads)
        query = q_all[tile(i)]
        entry = jnp.where(
            seg_col[tile(i), 0:1] == first_seg, jnp.exp(cum_col[tile(i), 0:1]), 0.0
        )
        carried = jnp.dot(query, pre_bf[...], preferred_element_type=F32)
        carried_n = jnp.sum(
            lax.dot_general(query, norm_two, (((1,), (1,)), ((), ())), preferred_element_type=F32),
            axis=1,
            keepdims=True,
        )
        bottom = qn[tile(i), 0:1] + entry * carried_n
        top = num[tile(i)] + entry * carried
        hid[tile(i)] = (top / jnp.maximum(jnp.abs(bottom), 1.0)).astype(BF16)
        for g in range(1, group):
            out_copy(i * group + lax.rem(m + g, group)).start()
        if d == 0:
            own_out().start()
        else:
            out_copy(i * group + m).start()

    finish_tile(1)
    finish_tile(0)
    for d in range(2, heads):
        take_query(d)
        take_others(d)
        query_tile(lax.rem(h + heads - d, heads))
        finish_tile(d)

    og_copy.wait()
    own_out().wait()

    def write_copy(hh):
        return pltpu.make_async_copy(
            out_v.at[:, head_cols(hh)], out_ref.at[:, head_cols(hh)], w_sem.at[hh]
        )

    def finish_head(step, carry):
        hh = lax.rem(h + step, heads)
        parts = []
        for g in range(group):
            b = hh * group + g

            @pl.when(b != t)
            def _():
                send(
                    hid.at[block(b)], out_rx.at[b], o_send.at[b], o_recv.at[b], "tensor", lax.rem(t + 1, ten_n)
                ).wait_recv()

            parts.append(out_rx[b].astype(F32))
        mean = sum(jnp.sum(x, axis=1, keepdims=True) for x in parts) * (1.0 / D)
        parts = [x - mean for x in parts]
        var = sum(jnp.sum(x * x, axis=1, keepdims=True) for x in parts) * (1.0 / D)
        inv = lax.rsqrt(var + EPS)
        for g in range(group):
            cols = val_cols(hh * group + g)
            gate = og_v[:, cols].astype(F32)
            silu = gate / (1.0 + jnp.exp(-gate))
            out_v[:, cols] = (parts[g] * inv * gain_ref[:, cols] * silu).astype(BF16)
        write_copy(hh).start()
        return carry

    lax.fori_loop(0, heads, finish_head, 0)

    for d in range(1, ten_n):
        gate_copy(d).wait_send()
        val_copy(d).wait_send()
        out_copy(lax.rem(t + d, ten_n)).wait_send()
    for d in range(1, heads):
        head_copy(q_ref, q_all, q_send, q_recv, d).wait_send()
        for c in range(nc):
            key_copy(d, c).wait_send()
    for g in range(1, group):
        own_forward(q_ref, q_all, q_fwd, q_recv, g).wait_send()
        for c in range(nc):
            for d in range(heads):
                key_forward(d, g, c).wait_send()
        for d in range(1, heads):
            forward(q_all, q_fwd, q_recv, d, g).wait_send()
    for d in range(1, seq_n):
        meta_copy(d).wait_send()
    for hh in range(heads):
        write_copy(hh).wait()
    for level in range(levels):
        norm_copy(level).wait_send()
        for c in range(nc):
            relay_copy(level, c).wait_send()


def on_device(
    seq_n, ten_n, queries, key_rows, values, input_gate, forget_gate, segment_ids, output_gate, norm_gain
):
    R, inner = queries.shape
    heads = input_gate.shape[1]
    D = inner // heads
    group = ten_n // heads
    C = D // group
    N = ten_n * R
    nc = D // min(256, D)
    levels = seq_n.bit_length() - 1
    lanes = max(R, 128)
    lines = 2 * heads
    segs = segment_ids.reshape(1, N)
    dma = pltpu.SemaphoreType.DMA
    vmem = pltpu.VMEM
    whole = pl.BlockSpec(memory_space=pltpu.VMEM)
    far = pl.BlockSpec(memory_space=pltpu.HBM)
    forwards = max(1, heads * (group - 1))
    return pl.pallas_call(
        functools.partial(kernel, (seq_n, ten_n, heads, R, D)),
        out_shape=jax.ShapeDtypeStruct((R, inner), BF16),
        in_specs=[whole, whole, far, far, far, far, far, far],
        out_specs=far,
        scratch_shapes=[
            vmem((lines, lanes), F32),
            vmem((ten_n, lines, lanes), F32),
            vmem((N, D), BF16),
            vmem((N, C), BF16),
            vmem((N, D), BF16),
            vmem((N, C), BF16),
            vmem((N, 128), F32),
            vmem((N, 128), F32),
            vmem((N, 128), F32),
            vmem((N, 128), F32),
            vmem((N, 128), F32),
            vmem((heads, 8, group * R), F32),
            vmem((8, 128), F32),
            vmem((seq_n, 8, 128), F32),
            vmem((D, C), F32),
            vmem((D, C), F32),
            vmem((D, C), BF16),
            vmem((levels, D, C), BF16),
            vmem((levels, D, C), BF16),
            vmem((8, D), F32),
            vmem((8, D), F32),
            vmem((levels, 8, D), F32),
            vmem((levels, 8, D), F32),
            vmem((N, C), F32),
            vmem((N, 128), F32),
            vmem((N, C), BF16),
            vmem((ten_n, R, C), BF16),
            vmem((R, inner), BF16),
            dma((ten_n,)),
            dma((ten_n,)),
            dma((heads, nc)),
            dma((forwards, nc)),
            dma((ten_n, nc)),
            dma((ten_n,)),
            dma((ten_n,)),
            dma((heads,)),
            dma((forwards,)),
            dma((ten_n,)),
            dma((seq_n,)),
            dma((seq_n,)),
            dma((levels, nc)),
            dma((levels, nc)),
            dma((levels,)),
            dma((levels,)),
            dma((ten_n,)),
            dma((ten_n,)),
            dma,
            dma,
            vmem((R, inner), BF16),
            dma((heads,)),
            vmem((1, N), jnp.int32),
            vmem((1, inner), F32),
            dma((2,)),
        ],
        compiler_params=pltpu.CompilerParams(
            collective_id=0, has_side_effects=True, vmem_limit_bytes=LIMIT
        ),
        cost_estimate=pl.CostEstimate(
            flops=2 * N * (N * D + N * C + 2 * D * C), bytes_accessed=10 * R * inner, transcendentals=N * N
        ),
    )(input_gate.T, forget_gate.T, segs, norm_gain.reshape(1, inner), queries, key_rows, values, output_gate)


def solution(mesh):
    rows = P(("seq", "tensor"), None)
    return jax.shard_map(
        functools.partial(on_device, mesh.shape["seq"], mesh.shape["tensor"]),
        mesh=mesh,
        in_specs=(rows, rows, rows, rows, rows, P("seq"), rows, P()),
        out_specs=rows,
        check_vma=False,
    )
```
